32 devices in a mesh: fft: 16 (over z, x, core), grp: 2 (over y).
Axes of the slice: x: 2, y: 2, z: 4, core: 2. Of those that a mesh axis runs over, the one named last changes fastest.
Arguments:
- psi_valence: bfloat16 [16, 64, 4096], P(None, 'fft'), may hold values from -6 to 6
- psi_conduction: bfloat16 [384, 64, 4096], P(None, 'fft'), may hold values from -6 to 6
- energy_valence: float32 [16], replicated, may hold values from -6 to -0.5
- energy_conduction: float32 [384], replicated, may hold values from 0.5 to 8
- pair_valence: int32 [80], P('grp'), may hold values from 0 to 15
- pair_conduction: int32 [80], P('grp'), may hold values from 0 to 383
- g_index: int32 [6144], replicated, may hold values from 0 to 262143, as said below
Outputs:
- chi_real: float32 [6144, 6144], P('fft', 'grp')
- chi_imag: float32 [6144, 6144], P('fft', 'grp')
The draws below stay inside these ranges and needn't reach their ends.
Inputs may be any that keep to these rules, and one draw needn't show every extreme that they name: `g_index`: the 6144 entries are distinct grid points in flat order a * 64 * 64 + b * 64 + c.
All inputs are finite; a program needn't handle non-finite values.
Results may differ from the reference program's by a relative error of at most 0.0041.
Values may be sent and summed in bfloat16 or wider, within the bound.
No kernel may reach another device: no remote copies, remote signals or barrier semaphores. Data moves between devices by JAX's collectives and lax.ppermute only.
A program may use at most 128 MiB of HBM per device.

```python
import jax
import jax.numpy as jnp
from jax import lax

NG = 64
V = 16
C = 384
NGV = 6144
ALL_PAIRS = 80


def draw_g_index(key, part):
    key = jax.random.fold_in(key, 7)
    perm_key, order_key = jax.random.split(key)
    grid_total = NG * NG * NG
    interior = jax.random.permutation(perm_key, grid_total - 2)[:NGV - 2].astype(jnp.int32) + 1
    chosen = jnp.concatenate([jnp.array([0, grid_total - 1], dtype=jnp.int32), interior])
    return jax.random.permutation(order_key, chosen).astype(jnp.int32)


def plant(entries, rng, least, high):
    longest = entries.shape.index(max(entries.shape))
    spots = []
    for shift in (0, 1):
        where = [jax.random.randint(jax.random.fold_in(rng, axis), (), 0, length) for axis, length in enumerate(entries.shape)]
        where[longest] = (where[longest] + shift) % entries.shape[longest]
        spots.append(tuple(where))
    return entries.at[spots[0]].set(least).at[spots[1]].set(high)


def level_of(key, extent, cuts, low, top_value):
    level = 1.0
    for dim, parts in cuts:
        draws = jax.random.uniform(jax.random.fold_in(jax.random.fold_in(key, 6), dim), (parts,), jnp.float32, low / len(cuts), top_value / len(cuts))
        level = level * jnp.repeat(jnp.exp(draws), extent[dim] // parts).reshape((-1,) + (1,) * (len(extent) - 1 - dim))
    return level


def centred(key, dims, width, limit, pieces=(), held_as=jnp.bfloat16):
    result = jax.random.normal(key, dims, jnp.float32) * width
    if len(pieces) > 0:
        result = level_of(key, dims, pieces, -0.22, 0.18) * result
    return jnp.clip(result, min=-limit, max=limit).astype(held_as)


def setup_inputs(seed: int = 0) -> dict:
    key_list = jax.random.split(jax.random.key(seed), 8)
    psi_valence = centred(key_list[0], (V, NG, NG * NG), 1.0, 6.0, ((1, 16),))
    psi_conduction = centred(key_list[1], (C, NG, NG * NG), 1.0, 6.0, ((1, 16),))
    energy_valence = jnp.clip(jax.random.uniform(key_list[2], (V,), jnp.float32, -6.0, -0.5), -6.0, -0.5)
    energy_conduction = jnp.clip(jax.random.uniform(key_list[3], (C,), jnp.float32, 0.5, 8.0), 0.5, 8.0)
    pair_valence = plant(jax.random.randint(key_list[4], (ALL_PAIRS,), 0, V), jax.random.fold_in(key_list[4], 1), 0, V - 1).astype(jnp.int32)
    pair_conduction = plant(jax.random.randint(key_list[5], (ALL_PAIRS,), 0, C), jax.random.fold_in(key_list[5], 1), 0, C - 1).astype(jnp.int32)
    g_index = draw_g_index(jax.random.fold_in(key_list[7], 71), 0)
    return {"psi_valence": psi_valence, "psi_conduction": psi_conduction, "energy_valence": energy_valence, "energy_conduction": energy_conduction, "pair_valence": pair_valence, "pair_conduction": pair_conduction, "g_index": g_index}


def reference(psi_valence, psi_conduction, energy_valence, energy_conduction, pair_valence, pair_conduction, g_index):
    weight = 2.0 / (energy_conduction[pair_conduction] - energy_valence[pair_valence])
    factor = jnp.sqrt(weight) * ALL_PAIRS ** (-0.25) * NG ** (-1.5)

    def transform(band_pair):
        density = psi_valence[band_pair[0]].astype(jnp.float32) * psi_conduction[band_pair[1]].astype(jnp.float32)
        density = density.reshape(NG, NG, NG)
        spectrum = jnp.fft.fftn(density).reshape(-1)[g_index]
        return (jnp.real(spectrum), jnp.imag(spectrum))
    sphere_real, sphere_imag = lax.map(transform, (pair_valence, pair_conduction))
    scaled_real = (sphere_real * factor[:, None]).astype(jnp.bfloat16)
    scaled_imag = (sphere_imag * factor[:, None]).astype(jnp.bfloat16)
    stack_sum = jnp.concatenate([scaled_real, scaled_imag], 0)
    left_cross = jnp.concatenate([scaled_real, -scaled_imag], 0)
    right_cross = jnp.concatenate([scaled_imag, scaled_real], 0)
    chi_real = -jnp.dot(stack_sum.T, stack_sum, preferred_element_type=jnp.float32)
    chi_imag = jnp.dot(left_cross.T, right_cross, preferred_element_type=jnp.float32)
    return (chi_real, chi_imag)
```

```python
import functools
import math

import jax
import jax.numpy as jnp
import numpy as np
from jax import lax
from jax.experimental import pallas as pl
from jax.experimental.pallas import tpu as pltpu
from jax.sharding import PartitionSpec as P

LANES = 128
SLOT = 64
UNROLL = 8
BF16 = jnp.bfloat16
F32 = jnp.float32


def split_table(table):
    high = table.astype(np.float32).astype(jnp.bfloat16)
    low = (table - high.astype(np.float64)).astype(np.float32).astype(jnp.bfloat16)
    return high, low


def dft_tables(length, pair_count):
    half = length // 2 + 1
    group = 2 * LANES // length
    index = np.arange(length)
    angle = 2.0 * np.pi * (np.outer(index, index) % length) / length
    cosine, sine = np.cos(angle), np.sin(angle)
    z_table = np.zeros((half + half % 2, 2, group, group, length))
    for y in range(group):
        z_table[:half, 0, y, y, :] = cosine[:half]
        z_table[:half, 1, y, y, :] = -sine[:half]
    z_table = z_table.reshape(-1, group * length)
    y_table = np.zeros((2, length, length // group, 2, group))
    folded = lambda t: t.reshape(length, length // group, group)
    y_table[0, :, :, 0, :] = folded(cosine)
    y_table[0, :, :, 1, :] = folded(sine)
    y_table[1, :, :, 0, :] = folded(-sine)
    y_table[1, :, :, 1, :] = folded(cosine)
    y_table = y_table.reshape(2 * length, 2 * length)
    deep = [np.concatenate([high, high, low], 1) for high, low in map(split_table, (y_table, z_table))]
    tables = np.zeros((deep[0].shape[0] + deep[1].shape[0], deep[1].shape[1]), jnp.bfloat16)
    tables[: deep[0].shape[0], : deep[0].shape[1]] = deep[0]
    tables[deep[0].shape[0] :] = deep[1]
    pick = (np.arange(2 * LANES)[None, :] % SLOT == np.arange(pair_count)[:, None]).astype(jnp.bfloat16)
    return tables, pick


def split(values):
    high = values.astype(BF16)
    low = (values - high.astype(F32)).astype(BF16)
    return high, low


def dot_nt(left, right):
    return lax.dot_general(left, right, (((1,), (1,)), ((), ())), preferred_element_type=F32)


def transform_kernel(length, pair_count, info, psi_v, psi_c, source, plane, coef, *scratch):
    val, con, tables, density, rows_z, sems = scratch
    half = length // 2 + 1
    planes = psi_v.shape[1]
    chunks = density.shape[0]
    copies = [
        pltpu.make_async_copy(a, b, sems.at[pair_count + i]) for i, (a, b) in enumerate([(psi_v, val), (source, tables)])
    ]
    copies[0].start()

    def pair_copy(p):
        return pltpu.make_async_copy(psi_c.at[info[pair_count + p]], con.at[p], sems.at[p])

    for p in range(pair_count):
        pair_copy(p).start()
    copies[1].start()
    shape = (length, 4 * LANES)
    a = lax.broadcasted_iota(jnp.int32, shape, 0)
    lane = lax.broadcasted_iota(jnp.int32, shape, 1)
    x = lax.axis_index("fft") * planes + lane % (2 * LANES) // SLOT
    turn = a * x - length // 4 * (lane // (2 * LANES)) + length
    high, low = split(jnp.cos((turn % length).astype(F32) * (2.0 * math.pi / length)))
    coef[:length] = high
    coef[length:] = low
    copies[0].wait()
    for p in range(pair_count):
        pair_copy(p).wait()
        pair_density = con[p].astype(F32) * val[info[p]].astype(F32)
        for k in range(chunks):
            density[k, p * planes : (p + 1) * planes, :] = pair_density[:, k * LANES : (k + 1) * LANES]
    copies[1].wait()

    y_rows = 2 * length
    z_rows = half * 8

    def z_step(step, _):
        parts = []
        for k in range(2):
            blocks = []
            for x in range(planes):
                blocks.append(density[2 * step + k, pl.ds(x, pair_count, stride=planes), :])
                blocks.append(jnp.zeros((SLOT - pair_count, LANES), F32))
            blocks += [jnp.zeros((SLOT, LANES), F32)] * (4 - planes)
            parts.append(jnp.concatenate(blocks, 0))
        high, low = split(jnp.concatenate(parts, 1))
        result = dot_nt(tables[y_rows:, :], jnp.concatenate([high, low, high], 1))[:z_rows]
        rows_z[:, pl.ds(pl.multiple_of(step * 8, 8), 8), :] = result.reshape(half, 8, 2 * LANES)
        return 0

    lax.fori_loop(0, chunks // 2, z_step, 0, unroll=2)

    def y_step(c, _):
        high, low = split(rows_z[c])
        result = jnp.dot(
            tables[:y_rows, : 3 * y_rows], jnp.concatenate([high, low, high], 0), preferred_element_type=F32
        )
        for part in range(2):
            for xh in range(2):
                block = result[part * length : (part + 1) * length, xh * LANES : (xh + 1) * LANES]
                plane[pl.ds(c * (4 * length) + part * 2 + xh, length, stride=4), :] = block
        return 0

    lax.fori_loop(0, half, y_step, 0, unroll=3)


def transform(psi_v, psi_c, info, pair_count, tables):
    planes, plane_size = psi_v.shape[1], psi_v.shape[2]
    length = math.isqrt(plane_size)
    half = length // 2 + 1
    chunks = plane_size // LANES
    hbm = pl.BlockSpec(memory_space=pl.ANY)
    return pl.pallas_call(
        functools.partial(transform_kernel, length, pair_count),
        out_shape=[
            jax.ShapeDtypeStruct((half * length * 4, LANES), F32),
            jax.ShapeDtypeStruct((2 * length, 4 * LANES), BF16),
        ],
        in_specs=[pl.BlockSpec(memory_space=pltpu.SMEM)] + [hbm] * 3,
        out_specs=[pl.BlockSpec(memory_space=pltpu.VMEM)] * 2,
        scratch_shapes=[
            pltpu.VMEM(psi_v.shape, BF16),
            pltpu.VMEM((pair_count, planes, plane_size), BF16),
            pltpu.VMEM(tables.shape, BF16),
            pltpu.VMEM((chunks, pair_count * planes, LANES), F32),
            pltpu.VMEM((half, 2 * length, 2 * LANES), F32),
            pltpu.SemaphoreType.DMA((pair_count + 2,)),
        ],
        compiler_params=pltpu.CompilerParams(vmem_limit_bytes=46 * 2**20),
        name="transform",
    )(info, psi_v, psi_c, tables)


def landing(chip, chips):
    return chip * 2 % chips + chip // (chips // 2)


def points_kernel(length, pair_count, planes, width, order, info, phase, plane, coef, pick, *refs):
    out, tiles_0, tiles_1, peak = refs[-4:]
    me = lax.axis_index("fft")
    blocks, rows = out.shape[0], out.shape[1]
    chunked = order is not None
    peak[...] = jnp.zeros_like(peak)
    which = lax.broadcasted_iota(jnp.int32, (2 * length, width), 0) % length

    def index_of(block):
        if not chunked:
            return block
        far, across = order
        half = lax.rem(lax.rem(me, 2) + far, 2)
        chips = phase.shape[0] // 2
        return half * chips + landing(jnp.bitwise_xor(me // 2, 2 * block + across), chips)

    def gather(block, tiles):
        first = 2 * pair_count + index_of(block) * width
        for start in range(0, width, UNROLL):
            loaded = [plane[info[first + start + u]] for u in range(UNROLL)]
            for u in range(UNROLL):
                tiles[(start + u) * 4 : (start + u + 1) * 4, :] = loaded[u]

    def combine(block, tiles):
        turns = phase[index_of(block)]
        one_hot = jnp.where(which == turns % length, 1.0, 0.0).astype(BF16)
        factors = lax.dot_general(
            one_hot, coef[...], (((0,), (0,)), ((), ())), preferred_element_type=F32
        )
        cos = [factors[:, k * LANES : (k + 1) * LANES] for k in range(2)]
        sin = [factors[:, (k + 2) * LANES : (k + 3) * LANES] for k in range(2)]
        real = [tiles[pl.ds(k, width, stride=4), :] for k in range(2)]
        imag = [tiles[pl.ds(k + 2, width, stride=4), :] for k in range(2)]
        sums = (
            cos[0] * real[0] + sin[0] * imag[0] + (cos[1] * real[1] + sin[1] * imag[1]),
            cos[0] * imag[0] - sin[0] * real[0] + (cos[1] * imag[1] - sin[1] * real[1]),
        )
        sign = jnp.where(turns >= length, -1.0, 1.0)
        for to_imag in range(2):
            high, low = split(sums[to_imag])
            result = dot_nt(pick[...], jnp.concatenate([high, low], 1))
            if to_imag:
                result = result * sign
            if not chunked:
                out[block, to_imag * pair_count : (to_imag + 1) * pair_count, :] = result
                continue
            for k in range(width // LANES):
                start = (2 * k + to_imag) * pair_count
                tile = result[:, k * LANES : (k + 1) * LANES]
                out[block, start : start + pair_count, :] = tile
                peak[...] = jnp.maximum(peak[...], jnp.abs(tile))

    gather(0, tiles_0)

    def two_blocks(step, _):
        block = 2 * step
        gather(block + 1, tiles_1)
        combine(block, tiles_0)
        gather(jnp.minimum(block + 2, blocks - 1), tiles_0)
        combine(block + 1, tiles_1)
        return 0

    lax.fori_loop(0, blocks // 2, two_blocks, 0)
    if chunked:
        used = width // LANES * 2 * pair_count
        top = jnp.full((rows - used, LANES), jnp.max(peak[...]))
        for block in range(blocks):
            out[block, used:, :] = top


def points(plane, coef, pick, info, phase, length, pair_count, planes, out_shape, order, after):
    after = () if after is None else (after,)
    width = phase.shape[2]
    vmem = pl.BlockSpec(memory_space=pltpu.VMEM)
    return pl.pallas_call(
        functools.partial(points_kernel, length, pair_count, planes, width, order),
        out_shape=jax.ShapeDtypeStruct(out_shape, F32),
        in_specs=[pl.BlockSpec(memory_space=pltpu.SMEM)]
        + [vmem] * 4
        + [pl.BlockSpec(memory_space=pl.ANY)] * len(after),
        out_specs=vmem,
        scratch_shapes=[
            pltpu.VMEM((width * 4, LANES), F32),
            pltpu.VMEM((width * 4, LANES), F32),
            pltpu.VMEM((pair_count, LANES), F32),
        ],
        compiler_params=pltpu.CompilerParams(vmem_limit_bytes=12 * 2**20),
        cost_estimate=pl.CostEstimate(flops=10**9 * out_shape[0], bytes_accessed=2**20, transcendentals=0),
        name="points",
    )(info, phase, plane, coef, pick, *after)


def sphere_parts(psi_v, psi_c, pair_v, pair_c, g_index, devices, paired):
    planes, plane_size = psi_v.shape[1], psi_v.shape[2]
    length = math.isqrt(plane_size)
    pair_count = pair_v.shape[0]
    width = g_index.shape[0] // devices
    a, b, c = g_index // plane_size, g_index // length % length, g_index % length
    flip = c > length // 2
    mirrored = lambda k: jnp.where(flip, (length - k) % length, k)
    spot = mirrored(c) * length + mirrored(b)
    phase = (mirrored(a) + jnp.where(flip, length, 0)).reshape(devices, 1, width)
    info = jnp.concatenate([pair_v, pair_c, spot])
    tables, pick = dft_tables(length, pair_count)
    plane, coef = transform(psi_v, psi_c, info, pair_count, tables)
    rest = (plane.reshape(-1, 4, LANES), coef, pick, info, phase, length, pair_count, planes)
    if not paired:
        return points(*rest, (devices, 2 * pair_count, width), None, None)
    size = (width // LANES * 2 * pair_count + 16, LANES)
    quarter = devices // 4
    return [
        functools.partial(points, *rest, (quarter, *size), order)
        for order in ((1, 1), (0, 1), (1, 0), (0, 0))
    ]


def chi_kernel(groups, pair_count, first, rows, cols, real, imag, left):
    width = rows.shape[1]

    @pl.when(pl.program_id(0) == 0)
    def _():
        own = rows[...].astype(F32)
        cross = []
        for group in range(groups):
            start = group * 2 * pair_count
            cross.append(-own[start + pair_count : start + 2 * pair_count])
            cross.append(own[start : start + pair_count])
        left[:width] = (-own).T.astype(BF16)
        left[width:] = jnp.concatenate(cross, 0).T.astype(BF16)

    for k in range(cols.shape[0]):
        both = jnp.dot(left[...], cols[k], preferred_element_type=F32)
        real[:, k * width : (k + 1) * width] = both[:width]
        imag[:, k * width : (k + 1) * width] = both[width:]


def chi_blocks(rows, cols, first, blocks, groups, pair_count):
    depth, width = rows.shape
    out = jax.ShapeDtypeStruct((width, blocks * width), F32)
    step = LANES // math.gcd(width, LANES)
    out_spec = pl.BlockSpec((width, step * width), lambda j, first: (0, j))
    return pl.pallas_call(
        functools.partial(chi_kernel, groups, pair_count),
        out_shape=(out, out),
        grid_spec=pltpu.PrefetchScalarGridSpec(
            num_scalar_prefetch=1,
            grid=(blocks // step,),
            in_specs=[
                pl.BlockSpec((depth, width), lambda j, first: (0, 0)),
                pl.BlockSpec((step, depth, width), lambda j, first: (first[0] // step + j, 0, 0)),
            ],
            out_specs=(out_spec, out_spec),
            scratch_shapes=[pltpu.VMEM((2 * width, depth), BF16)],
        ),
        compiler_params=pltpu.CompilerParams(vmem_limit_bytes=32 * 2**20),
        name="chi",
    )(first, rows, cols)


def chi_direct_kernel(pair_count, width, skip, has_left, *refs):
    depth = 2 * pair_count
    chunks = width // LANES
    wide = lambda piece: jnp.concatenate([piece[k * depth : (k + 1) * depth] for k in range(chunks)], 1)
    chip, chips = lax.axis_index("fft") // 2, lax.axis_size("fft") // 2
    if has_left:
        left, refs = refs[0], refs[3:]
    else:
        row_refs, refs = refs[:2], refs[2:]
    cols, refs = refs[:2], refs[2:]
    count = cols[0].shape[0]
    real, imag, *refs = refs
    if not has_left:
        left, *refs = refs
        own = [wide(piece[...].astype(F32)) for piece in row_refs]
        cross = [part for piece in own for part in (-piece[pair_count:], piece[:pair_count])]
        left[:width] = (-jnp.concatenate(own, 0)).T.astype(BF16)
        left[width:] = jnp.concatenate(cross, 0).T.astype(BF16)
    stage, sems = refs

    def copies(s):
        block = landing(jnp.bitwise_xor(chip, 2 * s + skip), chips)
        start = pl.multiple_of(block * width, LANES)
        return [
            pltpu.make_async_copy(
                stage.at[s, pl.ds(i * width, width)], out.at[:, pl.ds(start, width)], sems.at[s, i]
            )
            for i, out in enumerate((real, imag))
        ]

    for s in range(count):
        right = jnp.concatenate([wide(cols[i][s][...]) for i in range(2)], 0)
        stage[s] = jnp.dot(left[...], right, preferred_element_type=F32)
        for copy in copies(s):
            copy.start()
    for s in range(count):
        for copy in copies(s):
            copy.wait()


def chi_direct(rows, cols, skip, done, pair_count, width, blocks):
    count = cols[0].shape[0]
    out = jax.ShapeDtypeStruct((width, blocks * width), F32)
    left = jax.ShapeDtypeStruct((2 * width, 4 * pair_count), BF16)
    vmem = pl.BlockSpec(memory_space=pltpu.VMEM)
    hbm = pl.BlockSpec(memory_space=pl.ANY)
    if done is None:
        args, specs, aliases = rows, [vmem, vmem], {}
        out_shape, out_specs = (out, out, left), (hbm, hbm, vmem)
    else:
        real, imag, left = done
        args, specs, aliases = (left, real, imag), [vmem, hbm, hbm], {1: 0, 2: 1}
        out_shape, out_specs = (out, out), (hbm, hbm)
    return pl.pallas_call(
        functools.partial(chi_direct_kernel, pair_count, width, skip, done is not None),
        out_shape=out_shape,
        in_specs=specs + [vmem] * 2,
        out_specs=out_specs,
        scratch_shapes=[
            pltpu.VMEM((count, 2 * width, width), F32),
            pltpu.SemaphoreType.DMA((count, 2)),
        ],
        input_output_aliases=aliases,
        compiler_params=pltpu.CompilerParams(vmem_limit_bytes=32 * 2**20),
        cost_estimate=pl.CostEstimate(
            flops=8 * count * width * width * pair_count * 2,
            bytes_accessed=8 * count * width * width,
            transcendentals=0,
        ),
        name="chi",
    )(*args, *cols)


def pair_factor(energy_v, energy_c, pair_v, pair_c, length):
    chosen = lambda table, which: jnp.sum(
        jnp.where(which[:, None] == jnp.arange(table.shape[0])[None, :], table[None, :], 0.0), 1
    )
    weight = 2.0 / (chosen(energy_c, pair_c) - chosen(energy_v, pair_v))
    return jnp.sqrt(weight) * (pair_v.shape[0] * lax.axis_size("grp")) ** (-0.25) * length ** (-1.5)


def permute(values, moves):
    chips = lax.axis_size("fft") // 2
    perm = []
    for chip in range(chips):
        for core in range(2):
            for y in range(2):
                to_chip, to_core, to_y = moves(chip, core, y)
                perm.append((chip * 4 + core * 2 + y, to_chip * 4 + to_core * 2 + to_y))
    return lax.ppermute(values, ("fft", "grp"), perm)


def encode(values, used):
    top = values[..., used : used + 1, :]
    exponent = jnp.ceil(jnp.log2(jnp.maximum(top, 2.0**-100))) - 14.0
    row = lax.broadcasted_iota(jnp.int32, values.shape, values.ndim - 2)
    return jnp.where(row < used, values * jnp.exp2(-exponent), exponent).astype(jnp.float16)


def decode(coded, used):
    scale = jnp.exp2(coded[..., used : used + 1, :].astype(F32))
    row = lax.broadcasted_iota(jnp.int32, coded.shape, coded.ndim - 2)
    return jnp.where(row < used, coded.astype(F32), 2.0**14) * scale


def two_groups(psi_v, psi_c, energy_v, energy_c, pair_v, pair_c, g_index):
    devices = lax.axis_size("fft")
    chips = devices // 2
    quarter = chips // 2
    length = math.isqrt(psi_v.shape[2])
    pair_count = pair_v.shape[0]
    width = g_index.shape[0] // devices
    chunks = width // LANES
    used = chunks * 2 * pair_count
    fft, grp = lax.axis_index("fft"), lax.axis_index("grp")
    factor = pair_factor(energy_v, energy_c, pair_v, pair_c, length)
    factor = jnp.tile(factor, 2 * chunks)[:, None]
    swap = lambda values: permute(values, lambda chip, core, y: (chip, 1 - core, y))
    swap_x = lambda values: permute(values, lambda chip, core, y: (chip ^ 1, core, y))

    calls = sphere_parts(psi_v, psi_c, pair_v, pair_c, g_index, devices, True)
    far_x = calls[0](None)
    arrived = swap(far_x)
    across = calls[1](far_x) + arrived
    coded, across = lax.optimization_barrier((encode(across, used), across))
    arrived_x = swap_x(coded)
    far = calls[2](across)
    arrived = swap(far)
    kept = calls[3](far) + arrived + decode(arrived_x, used)
    total = kept[0]
    for s in range(1, quarter):
        move = lambda chip, core, y, s=s: (chip ^ (2 * s), core, y)
        total = total + decode(permute(encode(kept[s], used), move), used)
    own = (total[:used] * factor).astype(BF16)

    first = jnp.stack(
        [permute(own, lambda chip, core, y, s=s: (chip ^ (2 * s), y, core)) for s in range(quarter)]
    )
    first_x = swap_x(first)
    second = swap(first)

    def row_home(chip, core):
        return chip % quarter + core * quarter, chip // quarter

    same = permute(own, lambda chip, core, y: (*row_home(chip, core), y))
    cross = permute(own, lambda chip, core, y: (*row_home(chip, core), 1 - y))
    agree = fft % 2 == grp
    rows = (jnp.where(agree, same, cross), jnp.where(agree, cross, same))
    done = chi_direct(rows, (first, second), 0, None, pair_count, width, chips)
    first_x, left = lax.optimization_barrier((first_x, done[2]))
    second_x = swap(first_x)
    done = (*done[:2], left)
    return chi_direct(None, (first_x, second_x), 1, done, pair_count, width, chips)


def any_groups(psi_v, psi_c, energy_v, energy_c, pair_v, pair_c, g_index):
    devices, groups = lax.axis_size("fft"), lax.axis_size("grp")
    length = math.isqrt(psi_v.shape[2])
    pair_count = pair_v.shape[0]
    parts = sphere_parts(psi_v, psi_c, pair_v, pair_c, g_index, devices, False)
    factor = pair_factor(energy_v, energy_c, pair_v, pair_c, length)
    factor = jnp.concatenate([factor, factor])
    arrived = lax.all_to_all(parts, "fft", split_axis=0, concat_axis=0, tiled=True)
    own = (jnp.sum(arrived, 0) * factor[:, None]).astype(BF16)
    rows = lax.all_gather(own, "grp", axis=0, tiled=True)
    cols = lax.all_gather(rows, "fft", axis=0, tiled=False)
    blocks = devices // groups
    first = (lax.axis_index("grp") * blocks).astype(jnp.int32).reshape(1)
    return chi_blocks(rows, cols, first, blocks, groups, pair_count)


def per_device(
    psi_valence,
    psi_conduction,
    energy_valence,
    energy_conduction,
    pair_valence,
    pair_conduction,
    g_index,
):
    args = (
        psi_valence,
        psi_conduction,
        energy_valence,
        energy_conduction,
        pair_valence,
        pair_conduction,
        g_index,
    )
    devices = lax.axis_size("fft")
    chips = devices // 2
    power_of_two = devices % 2 == 0 and chips & (chips - 1) == 0
    if lax.axis_size("grp") == 2 and power_of_two and chips >= 4 and g_index.shape[0] % (devices * LANES) == 0:
        return two_groups(*args)
    return any_groups(*args)


def solution(mesh):
    placed = (P(None, "fft", None), P(None, "fft", None), P(), P(), P("grp"), P("grp"), P())
    return jax.shard_map(
        per_device,
        mesh=mesh,
        in_specs=placed,
        out_specs=(P("fft", "grp"), P("fft", "grp")),
        check_vma=False,
    )
```

```python
import functools
import math

import jax
import jax.numpy as jnp
import numpy as np
from jax import lax
from jax.experimental import pallas as pl
from jax.experimental.pallas import tpu as pltpu
from jax.sharding import PartitionSpec as P

LANES = 128
SLOT = 64
UNROLL = 8
BF16 = jnp.bfloat16
F32 = jnp.float32


def cosine(turn, length):
    from_half = jnp.abs(turn - length // 2)
    folded = jnp.minimum(from_half, length // 2 - from_half)
    square = (folded.astype(F32) * (2.0 * math.pi / length)) ** 2
    value = jnp.full(square.shape, 1.0 / math.factorial(12), F32)
    for order in range(10, -1, -2):
        value = value * square + (-1.0) ** (order // 2) / math.factorial(order)
    return jnp.where(from_half > length // 4, value, -value)


def split(values):
    high = values.astype(BF16)
    low = (values - high.astype(F32)).astype(BF16)
    return high, low


def dot_nt(left, right):
    return lax.dot_general(left, right, (((1,), (1,)), ((), ())), preferred_element_type=F32)


def fill_tables(length, planes, z_table, y_table, coef):
    quarter = length // 4
    group = 2 * LANES // length

    def put(table, values):
        high, low = split(values)
        for k, part in enumerate((high, high, low)):
            table[:, k * values.shape[1] : (k + 1) * values.shape[1]] = part

    shape = (z_table.shape[0], group * length)
    row, column = (lax.broadcasted_iota(jnp.int32, shape, axis) for axis in range(2))
    c, to_imag, y = row // (2 * group), row // group % 2, row % group
    value = cosine((c * (column % length) + quarter * to_imag) % length, length)
    put(z_table, jnp.where(column // length == y, value, 0.0))
    shape = (2 * length, 2 * length)
    row, column = (lax.broadcasted_iota(jnp.int32, shape, axis) for axis in range(2))
    y, from_imag = column // (2 * group) * group + column % group, column // group % 2
    turn = row % length * y + quarter * (row // length - from_imag) + length
    put(y_table, cosine(turn % length, length))
    shape = (length, 4 * LANES)
    a, lane = (lax.broadcasted_iota(jnp.int32, shape, axis) for axis in range(2))
    x = lax.axis_index("fft") * planes + lane % (2 * LANES) // SLOT
    turn = a * x - quarter * (lane // (2 * LANES)) + length
    high, low = split(cosine(turn % length, length))
    coef[:length] = high
    coef[length:] = low


def transform_kernel(length, pair_count, info, g_index, psi_v, psi_c, plane, coef, spot, phase, *scratch):
    val, con, z_table, y_table, chunk_0, chunk_1, rows_z, sems = scratch
    half = length // 2 + 1
    planes = psi_v.shape[1]
    steps = psi_v.shape[2] // (2 * LANES)

    def pair_copy(p):
        return pltpu.make_async_copy(psi_c.at[info[pair_count + p]], con.at[p], sems.at[p])

    for p in range(pair_count):
        pair_copy(p).start()
    fill_tables(length, planes, z_table, y_table, coef)
    points = g_index[...]
    a, b, c = points // (length * length), points // length % length, points % length
    flip = c > length // 2
    mirrored = lambda k: jnp.where(flip, (length - k) % length, k)
    spot[...] = mirrored(c) * length + mirrored(b)
    phase[...] = mirrored(a) + jnp.where(flip, length, 0)
    val[...] = psi_v[...].astype(F32)
    for p in range(pair_count):
        pair_copy(p).wait()

    def density(step, chunk):
        lanes = pl.ds(pl.multiple_of(step * (2 * LANES), 2 * LANES), 2 * LANES)
        for p in range(pair_count):
            values = con[p, :, lanes].astype(F32) * val[info[p], :, lanes]
            for k in range(2):
                chunk[k, p * planes : (p + 1) * planes, :] = values[:, k * LANES : (k + 1) * LANES]

    def z_step(step, chunk):
        parts = []
        for k in range(2):
            blocks = []
            for x in range(planes):
                blocks.append(chunk[k, pl.ds(x, pair_count, stride=planes), :])
                blocks.append(jnp.zeros((SLOT - pair_count, LANES), F32))
            blocks += [jnp.zeros((SLOT, LANES), F32)] * (4 - planes)
            parts.append(jnp.concatenate(blocks, 0))
        high, low = split(jnp.concatenate(parts, 1))
        result = dot_nt(z_table[...], jnp.concatenate([high, low, high], 1))[: half * 8]
        rows_z[:, pl.ds(pl.multiple_of(step * 8, 8), 8), :] = result.reshape(half, 8, 2 * LANES)

    density(0, chunk_0)

    def two_steps(i, _):
        density(2 * i + 1, chunk_1)
        z_step(2 * i, chunk_0)
        density(jnp.minimum(2 * i + 2, steps - 1), chunk_0)
        z_step(2 * i + 1, chunk_1)
        return 0

    lax.fori_loop(0, steps // 2, two_steps, 0)

    def y_step(c, _):
        high, low = split(rows_z[c])
        result = jnp.dot(y_table[...], jnp.concatenate([high, low, high], 0), preferred_element_type=F32)
        for part in range(2):
            for xh in range(2):
                block = result[part * length : (part + 1) * length, xh * LANES : (xh + 1) * LANES]
                plane[pl.ds(c * (4 * length) + part * 2 + xh, length, stride=4), :] = block
        return 0

    lax.fori_loop(0, half, y_step, 0, unroll=3)


def transform(psi_v, psi_c, info, pair_count, g_index):
    planes, plane_size = psi_v.shape[1], psi_v.shape[2]
    length = math.isqrt(plane_size)
    half = length // 2 + 1
    vmem = pl.BlockSpec(memory_space=pltpu.VMEM)
    index = jax.ShapeDtypeStruct(g_index.shape, jnp.int32)
    return pl.pallas_call(
        functools.partial(transform_kernel, length, pair_count),
        out_shape=[
            jax.ShapeDtypeStruct((half * length * 4, LANES), F32),
            jax.ShapeDtypeStruct((2 * length, 4 * LANES), BF16),
            index,
            index,
        ],
        in_specs=[pl.BlockSpec(memory_space=pltpu.SMEM), vmem, vmem, pl.BlockSpec(memory_space=pl.ANY)],
        out_specs=[vmem] * 4,
        scratch_shapes=[
            pltpu.VMEM(psi_v.shape, F32),
            pltpu.VMEM((pair_count, planes, plane_size), BF16),
            pltpu.VMEM(((half + half % 2) * 8, 6 * LANES), BF16),
            pltpu.VMEM((2 * length, 6 * length), BF16),
            pltpu.VMEM((2, pair_count * planes, LANES), F32),
            pltpu.VMEM((2, pair_count * planes, LANES), F32),
            pltpu.VMEM((half, 2 * length, 2 * LANES), F32),
            pltpu.SemaphoreType.DMA((pair_count,)),
        ],
        compiler_params=pltpu.CompilerParams(vmem_limit_bytes=40 * 2**20),
        name="transform",
    )(info, g_index, psi_v, psi_c)


def landing(chip, chips):
    return chip * 2 % chips + chip // (chips // 2)


def points_kernel(length, pair_count, width, orders, spot, phase, plane, coef, pick, *refs):
    *refs, tiles_0, tiles_1, peak, local, sems = refs
    outs = refs[-max(len(orders), 1) :]
    me = lax.axis_index("fft")
    blocks, rows = outs[0].shape[0], outs[0].shape[1]
    last = blocks * len(outs) - 1
    chunked = len(orders) > 0
    which = lax.broadcasted_iota(jnp.int32, (2 * length, width), 0) % length

    def index_of(block):
        if not chunked:
            return block
        group, block = block // blocks, block % blocks
        far, across = (
            sum(jnp.where(group == k, order[axis], 0) for k, order in enumerate(orders)) for axis in range(2)
        )
        half = lax.rem(lax.rem(me, 2) + far, 2)
        chips = phase.shape[0] // 2
        return half * chips + landing(jnp.bitwise_xor(me // 2, 2 * block + across), chips)

    def fetch(block):
        return pltpu.make_async_copy(spot.at[index_of(block)], local.at[block], sems.at[block])

    def gather(block, tiles):
        for start in range(0, width, UNROLL):
            loaded = [plane[local[block, 0, start + u]] for u in range(UNROLL)]
            for u in range(UNROLL):
                tiles[(start + u) * 4 : (start + u + 1) * 4, :] = loaded[u]

    def combine(group, block, tiles):
        out = outs[group]
        turns = phase[index_of(group * blocks + block)]
        one_hot = jnp.where(which == turns % length, 1.0, 0.0).astype(BF16)
        factors = lax.dot_general(
            one_hot, coef[...], (((0,), (0,)), ((), ())), preferred_element_type=F32
        )
        cos = [factors[:, k * LANES : (k + 1) * LANES] for k in range(2)]
        sin = [factors[:, (k + 2) * LANES : (k + 3) * LANES] for k in range(2)]
        real = [tiles[pl.ds(k, width, stride=4), :] for k in range(2)]
        imag = [tiles[pl.ds(k + 2, width, stride=4), :] for k in range(2)]
        sums = (
            cos[0] * real[0] + sin[0] * imag[0] + (cos[1] * real[1] + sin[1] * imag[1]),
            cos[0] * imag[0] - sin[0] * real[0] + (cos[1] * imag[1] - sin[1] * real[1]),
        )
        sign = jnp.where(turns >= length, -1.0, 1.0)
        for to_imag in range(2):
            high, low = split(sums[to_imag])
            result = dot_nt(pick[...], jnp.concatenate([high, low], 1))
            if to_imag:
                result = result * sign
            if not chunked:
                out[block, to_imag * pair_count : (to_imag + 1) * pair_count, :] = result
                continue
            for k in range(width // LANES):
                start = (2 * k + to_imag) * pair_count
                tile = result[:, k * LANES : (k + 1) * LANES]
                out[block, start : start + pair_count, :] = tile
                peak[...] = jnp.maximum(peak[...], jnp.abs(tile))

    for block in range(last + 1):
        fetch(block).start()
    peak[...] = jnp.zeros_like(peak)
    fetch(0).wait()
    gather(0, tiles_0)
    for block in range(1, last + 1):
        fetch(block).wait()
    for group in range(len(outs)):

        def two_blocks(step, _):
            block = group * blocks + 2 * step
            gather(block + 1, tiles_1)
            combine(group, 2 * step, tiles_0)
            gather(jnp.minimum(block + 2, last), tiles_0)
            combine(group, 2 * step + 1, tiles_1)
            return 0

        lax.fori_loop(0, blocks // 2, two_blocks, 0)
    if chunked:
        used = width // LANES * 2 * pair_count
        top = jnp.full((rows - used, LANES), jnp.max(peak[...]))
        for out in outs:
            for block in range(blocks):
                out[block, used:, :] = top


def points(spot, phase, plane, coef, pick, pair_count, out_shape, orders, after):
    after = () if after is None else (after,)
    count = max(len(orders), 1)
    length, width = coef.shape[0] // 2, phase.shape[2]
    vmem = pl.BlockSpec(memory_space=pltpu.VMEM)
    hbm = pl.BlockSpec(memory_space=pl.ANY)
    return pl.pallas_call(
        functools.partial(points_kernel, length, pair_count, width, orders),
        out_shape=[jax.ShapeDtypeStruct(out_shape, F32)] * count,
        in_specs=[hbm] + [vmem] * 4 + [hbm] * len(after),
        out_specs=[vmem] * count,
        scratch_shapes=[
            pltpu.VMEM((width * 4, LANES), F32),
            pltpu.VMEM((width * 4, LANES), F32),
            pltpu.VMEM((pair_count, LANES), F32),
            pltpu.SMEM((count * out_shape[0], 1, width), jnp.int32),
            pltpu.SemaphoreType.DMA((count * out_shape[0],)),
        ],
        compiler_params=pltpu.CompilerParams(vmem_limit_bytes=12 * 2**20),
        cost_estimate=pl.CostEstimate(flops=10**8 * out_shape[0], bytes_accessed=2**20, transcendentals=0),
        name="points",
    )(spot, phase, plane, coef, pick, *after)


def sphere_parts(psi_v, psi_c, pair_v, pair_c, g_index, devices, paired):
    pair_count = pair_v.shape[0]
    width = g_index.shape[0] // devices
    info = jnp.concatenate([pair_v, pair_c])
    plane, coef, spot, phase = transform(psi_v, psi_c, info, pair_count, g_index.reshape(devices, 1, width))
    pick = (np.arange(2 * LANES)[None, :] % SLOT == np.arange(pair_count)[:, None]).astype(jnp.bfloat16)
    rest = (spot, phase, plane.reshape(-1, 4, LANES), coef, pick, pair_count)
    if not paired:
        return points(*rest, (devices, 2 * pair_count, width), (), None)[0]
    shape = (devices // 4, width // LANES * 2 * pair_count + 16, LANES)
    return [functools.partial(points, *rest, shape, orders) for orders in (((1, 1),), ((0, 1),), ((1, 0), (0, 0)))]


def chi_kernel(groups, pair_count, first, rows, cols, real, imag, left):
    width = rows.shape[1]

    @pl.when(pl.program_id(0) == 0)
    def _():
        own = rows[...].astype(F32)
        cross = []
        for group in range(groups):
            start = group * 2 * pair_count
            cross.append(-own[start + pair_count : start + 2 * pair_count])
            cross.append(own[start : start + pair_count])
        left[:width] = (-own).T.astype(BF16)
        left[width:] = jnp.concatenate(cross, 0).T.astype(BF16)

    for k in range(cols.shape[0]):
        both = jnp.dot(left[...], cols[k], preferred_element_type=F32)
        real[:, k * width : (k + 1) * width] = both[:width]
        imag[:, k * width : (k + 1) * width] = both[width:]


def chi_blocks(rows, cols, first, blocks, groups, pair_count):
    depth, width = rows.shape
    out = jax.ShapeDtypeStruct((width, blocks * width), F32)
    step = LANES // math.gcd(width, LANES)
    out_spec = pl.BlockSpec((width, step * width), lambda j, first: (0, j))
    return pl.pallas_call(
        functools.partial(chi_kernel, groups, pair_count),
        out_shape=(out, out),
        grid_spec=pltpu.PrefetchScalarGridSpec(
            num_scalar_prefetch=1,
            grid=(blocks // step,),
            in_specs=[
                pl.BlockSpec((depth, width), lambda j, first: (0, 0)),
                pl.BlockSpec((step, depth, width), lambda j, first: (first[0] // step + j, 0, 0)),
            ],
            out_specs=(out_spec, out_spec),
            scratch_shapes=[pltpu.VMEM((2 * width, depth), BF16)],
        ),
        compiler_params=pltpu.CompilerParams(vmem_limit_bytes=32 * 2**20),
        name="chi",
    )(first, rows, cols)


def chi_direct_kernel(pair_count, width, skip, has_left, *refs):
    depth = 2 * pair_count
    chunks = width // LANES
    wide = lambda piece: jnp.concatenate([piece[k * depth : (k + 1) * depth] for k in range(chunks)], 1)
    chip, chips = lax.axis_index("fft") // 2, lax.axis_size("fft") // 2
    if has_left:
        left, refs = refs[0], refs[3:]
    else:
        row_refs, refs = refs[:2], refs[2:]
    cols, refs = refs[:2], refs[2:]
    count = cols[0].shape[0]
    real, imag, *refs = refs
    if not has_left:
        left, *refs = refs
        own = [wide(piece[...].astype(F32)) for piece in row_refs]
        cross = [part for piece in own for part in (-piece[pair_count:], piece[:pair_count])]
        left[:width] = (-jnp.concatenate(own, 0)).T.astype(BF16)
        left[width:] = jnp.concatenate(cross, 0).T.astype(BF16)
    stage, sems = refs

    def copies(s):
        block = landing(jnp.bitwise_xor(chip, 2 * s + skip), chips)
        start = pl.multiple_of(block * width, LANES)
        return [
            pltpu.make_async_copy(
                stage.at[s, pl.ds(i * width, width)], out.at[:, pl.ds(start, width)], sems.at[s, i]
            )
            for i, out in enumerate((real, imag))
        ]

    for s in range(count):
        right = jnp.concatenate([wide(cols[i][s][...]) for i in range(2)], 0)
        stage[s] = jnp.dot(left[...], right, preferred_element_type=F32)
        for copy in copies(s):
            copy.start()
    for s in range(count):
        for copy in copies(s):
            copy.wait()


def chi_direct(rows, cols, skip, done, pair_count, width, blocks):
    count = cols[0].shape[0]
    out = jax.ShapeDtypeStruct((width, blocks * width), F32)
    left = jax.ShapeDtypeStruct((2 * width, 4 * pair_count), BF16)
    vmem = pl.BlockSpec(memory_space=pltpu.VMEM)
    hbm = pl.BlockSpec(memory_space=pl.ANY)
    if done is None:
        args, specs, aliases = rows, [vmem, vmem], {}
        out_shape, out_specs = (out, out, left), (hbm, hbm, vmem)
    else:
        real, imag, left = done
        args, specs, aliases = (left, real, imag), [vmem, hbm, hbm], {1: 0, 2: 1}
        out_shape, out_specs = (out, out), (hbm, hbm)
    return pl.pallas_call(
        functools.partial(chi_direct_kernel, pair_count, width, skip, done is not None),
        out_shape=out_shape,
        in_specs=specs + [vmem] * 2,
        out_specs=out_specs,
        scratch_shapes=[
            pltpu.VMEM((count, 2 * width, width), F32),
            pltpu.SemaphoreType.DMA((count, 2)),
        ],
        input_output_aliases=aliases,
        compiler_params=pltpu.CompilerParams(vmem_limit_bytes=32 * 2**20),
        cost_estimate=pl.CostEstimate(
            flops=8 * count * width * width * pair_count * 2,
            bytes_accessed=8 * count * width * width,
            transcendentals=0,
        ),
        name="chi",
    )(*args, *cols)


def pair_factor(energy_v, energy_c, pair_v, pair_c, length):
    chosen = lambda table, which: jnp.sum(
        jnp.where(which[:, None] == jnp.arange(table.shape[0])[None, :], table[None, :], 0.0), 1
    )
    weight = 2.0 / (chosen(energy_c, pair_c) - chosen(energy_v, pair_v))
    return jnp.sqrt(weight) * (pair_v.shape[0] * lax.axis_size("grp")) ** (-0.25) * length ** (-1.5)


def permute(values, moves):
    chips = lax.axis_size("fft") // 2
    perm = []
    for chip in range(chips):
        for core in range(2):
            for y in range(2):
                to_chip, to_core, to_y = moves(chip, core, y)
                perm.append((chip * 4 + core * 2 + y, to_chip * 4 + to_core * 2 + to_y))
    return lax.ppermute(values, ("fft", "grp"), perm)


def encode(values, used):
    top = values[..., used : used + 1, :]
    exponent = jnp.ceil(jnp.log2(jnp.maximum(top, 2.0**-100))) - 14.0
    row = lax.broadcasted_iota(jnp.int32, values.shape, values.ndim - 2)
    return jnp.where(row < used, values * jnp.exp2(-exponent), exponent).astype(jnp.float16)


def decode(coded, used):
    scale = jnp.exp2(coded[..., used : used + 1, :].astype(F32))
    row = lax.broadcasted_iota(jnp.int32, coded.shape, coded.ndim - 2)
    return jnp.where(row < used, coded.astype(F32), 2.0**14) * scale


def two_groups(psi_v, psi_c, energy_v, energy_c, pair_v, pair_c, g_index):
    devices = lax.axis_size("fft")
    chips = devices // 2
    quarter = chips // 2
    length = math.isqrt(psi_v.shape[2])
    pair_count = pair_v.shape[0]
    width = g_index.shape[0] // devices
    chunks = width // LANES
    used = chunks * 2 * pair_count
    fft, grp = lax.axis_index("fft"), lax.axis_index("grp")
    swap = lambda values: permute(values, lambda chip, core, y: (chip, 1 - core, y))
    swap_x = lambda values: permute(values, lambda chip, core, y: (chip ^ 1, core, y))

    calls = sphere_parts(psi_v, psi_c, pair_v, pair_c, g_index, devices, True)
    (far,) = calls[0](None)
    arrived = swap(far)
    (across,) = calls[1](far)
    across = across + arrived
    coded, across = lax.optimization_barrier((encode(across, used), across))
    arrived_x = swap_x(coded)
    far, kept = calls[2](across)
    arrived_x, far = lax.optimization_barrier((arrived_x, far))
    kept = kept + swap(far) + decode(arrived_x, used)
    (pair_v, pair_c), kept = lax.optimization_barrier(((pair_v, pair_c), kept))
    factor = pair_factor(energy_v, energy_c, pair_v, pair_c, length)
    factor = jnp.tile(factor, 2 * chunks)[:, None]
    total = kept[0]
    for s in reversed(range(1, quarter)):
        move = lambda chip, core, y, s=s: (chip ^ (2 * s), core, y)
        total = total + decode(permute(encode(kept[s], used), move), used)
    own = (total[:used] * factor).astype(BF16)

    first = jnp.stack(
        [permute(own, lambda chip, core, y, s=s: (chip ^ (2 * s), y, core)) for s in range(quarter)]
    )
    first_x = swap_x(first)
    second = swap(first)

    def row_home(chip, core):
        return chip % quarter + core * quarter, chip // quarter

    same = permute(own, lambda chip, core, y: (*row_home(chip, core), y))
    cross = permute(own, lambda chip, core, y: (*row_home(chip, core), 1 - y))
    agree = fft % 2 == grp
    rows = (jnp.where(agree, same, cross), jnp.where(agree, cross, same))
    done = chi_direct(rows, (first, second), 0, None, pair_count, width, chips)
    first_x, left = lax.optimization_barrier((first_x, done[2]))
    second_x = swap(first_x)
    done = (*done[:2], left)
    return chi_direct(None, (first_x, second_x), 1, done, pair_count, width, chips)


def any_groups(psi_v, psi_c, energy_v, energy_c, pair_v, pair_c, g_index):
    devices, groups = lax.axis_size("fft"), lax.axis_size("grp")
    length = math.isqrt(psi_v.shape[2])
    pair_count = pair_v.shape[0]
    parts = sphere_parts(psi_v, psi_c, pair_v, pair_c, g_index, devices, False)
    factor = pair_factor(energy_v, energy_c, pair_v, pair_c, length)
    factor = jnp.concatenate([factor, factor])
    arrived = lax.all_to_all(parts, "fft", split_axis=0, concat_axis=0, tiled=True)
    own = (jnp.sum(arrived, 0) * factor[:, None]).astype(BF16)
    rows = lax.all_gather(own, "grp", axis=0, tiled=True)
    cols = lax.all_gather(rows, "fft", axis=0, tiled=False)
    blocks = devices // groups
    first = (lax.axis_index("grp") * blocks).astype(jnp.int32).reshape(1)
    return chi_blocks(rows, cols, first, blocks, groups, pair_count)


def per_device(
    psi_valence,
    psi_conduction,
    energy_valence,
    energy_conduction,
    pair_valence,
    pair_conduction,
    g_index,
):
    args = (
        psi_valence,
        psi_conduction,
        energy_valence,
        energy_conduction,
        pair_valence,
        pair_conduction,
        g_index,
    )
    devices = lax.axis_size("fft")
    chips = devices // 2
    power_of_two = devices % 2 == 0 and chips & (chips - 1) == 0
    if lax.axis_size("grp") == 2 and power_of_two and chips >= 4 and g_index.shape[0] % (devices * LANES) == 0:
        return two_groups(*args)
    return any_groups(*args)


def solution(mesh):
    placed = (P(None, "fft", None), P(None, "fft", None), P(), P(), P("grp"), P("grp"), P())
    return jax.shard_map(
        per_device,
        mesh=mesh,
        in_specs=placed,
        out_specs=(P("fft", "grp"), P("fft", "grp")),
        check_vma=False,
    )
```

```python
import functools
import math

import jax
import jax.numpy as jnp
import numpy as np
from jax import lax
from jax.experimental import pallas as pl
from jax.experimental.pallas import tpu as pltpu
from jax.sharding import PartitionSpec as P

LANES = 128
SLOT = 64
UNROLL = 8
BF16 = jnp.bfloat16
F32 = jnp.float32


def cosine(turn, length):
    from_half = jnp.abs(turn - length // 2)
    folded = jnp.minimum(from_half, length // 2 - from_half)
    square = (folded.astype(F32) * (2.0 * math.pi / length)) ** 2
    value = jnp.full(square.shape, 1.0 / math.factorial(12), F32)
    for order in range(10, -1, -2):
        value = value * square + (-1.0) ** (order // 2) / math.factorial(order)
    return jnp.where(from_half > length // 4, value, -value)


def split(values):
    high = values.astype(BF16)
    low = (values - high.astype(F32)).astype(BF16)
    return high, low


def dot_nt(left, right):
    return lax.dot_general(left, right, (((1,), (1,)), ((), ())), preferred_element_type=F32)


def put(table, values):
    high, low = split(values)
    for k, part in enumerate((high, high, low)):
        table[:, k * values.shape[1] : (k + 1) * values.shape[1]] = part


def fill_z_table(length, z_table):
    quarter = length // 4
    group = 2 * LANES // length
    shape = (z_table.shape[0], group * length)
    row, column = (lax.broadcasted_iota(jnp.int32, shape, axis) for axis in range(2))
    c, to_imag, y = row // (2 * group), row // group % 2, row % group
    value = cosine((c * (column % length) + quarter * to_imag) % length, length)
    put(z_table, jnp.where(column // length == y, value, 0.0))


def fill_tables(length, planes, y_table, coef):
    quarter = length // 4
    group = 2 * LANES // length
    shape = (2 * length, 2 * length)
    row, column = (lax.broadcasted_iota(jnp.int32, shape, axis) for axis in range(2))
    y, from_imag = column // (2 * group) * group + column % group, column // group % 2
    turn = row % length * y + quarter * (row // length - from_imag) + length
    put(y_table, cosine(turn % length, length))
    shape = (length, 4 * LANES)
    a, lane = (lax.broadcasted_iota(jnp.int32, shape, axis) for axis in range(2))
    x = lax.axis_index("fft") * planes + lane % (2 * LANES) // SLOT
    turn = a * x - quarter * (lane // (2 * LANES)) + length
    high, low = split(cosine(turn % length, length))
    coef[:length] = high
    coef[length:] = low


def transform_kernel(length, pair_count, meta, psi_v, psi_c, plane, coef, spot, phase, *scratch):
    val, con, z_table, y_table, chunk_0, chunk_1, rows_z, pairs, sems = scratch
    width, count = meta.shape[2], spot.shape[0]
    pairs_copy = pltpu.make_async_copy(meta.at[pl.ds(count, pairs.shape[0])], pairs, sems.at[pair_count])
    pairs_copy.start()
    fill_z_table(length, z_table)
    pairs_copy.wait()
    valence = [pairs[p // width, 0, p % width] for p in range(pair_count)]
    conduction = [pairs[p // width, 0, p % width] for p in range(pair_count, 2 * pair_count)]
    half = length // 2 + 1
    planes = psi_v.shape[1]
    steps = psi_v.shape[2] // (2 * LANES)

    def pair_copy(p):
        return pltpu.make_async_copy(psi_c.at[conduction[p]], con.at[p], sems.at[p])

    for p in range(pair_count):
        pair_copy(p).start()
    fill_tables(length, planes, y_table, coef)
    points = meta[:count]
    a, b, c = points // (length * length), points // length % length, points % length
    flip = c > length // 2
    mirrored = lambda k: jnp.where(flip, (length - k) % length, k)
    spot[...] = mirrored(c) * length + mirrored(b)
    phase[...] = mirrored(a) + jnp.where(flip, length, 0)
    val[...] = psi_v[...].astype(F32)
    for p in range(pair_count):
        pair_copy(p).wait()

    def density(step, chunk):
        lanes = pl.ds(pl.multiple_of(step * (2 * LANES), 2 * LANES), 2 * LANES)
        for p in range(pair_count):
            values = con[p, :, lanes].astype(F32) * val[valence[p], :, lanes]
            for k in range(2):
                chunk[k, p * planes : (p + 1) * planes, :] = values[:, k * LANES : (k + 1) * LANES]

    def z_step(step, chunk):
        parts = []
        for k in range(2):
            blocks = []
            for x in range(planes):
                blocks.append(chunk[k, pl.ds(x, pair_count, stride=planes), :])
                blocks.append(jnp.zeros((SLOT - pair_count, LANES), F32))
            blocks += [jnp.zeros((SLOT, LANES), F32)] * (4 - planes)
            parts.append(jnp.concatenate(blocks, 0))
        high, low = split(jnp.concatenate(parts, 1))
        result = dot_nt(z_table[...], jnp.concatenate([high, low, high], 1))[: half * 8]
        rows_z[:, pl.ds(pl.multiple_of(step * 8, 8), 8), :] = result.reshape(half, 8, 2 * LANES)

    density(0, chunk_0)

    def two_steps(i, _):
        density(2 * i + 1, chunk_1)
        z_step(2 * i, chunk_0)
        density(jnp.minimum(2 * i + 2, steps - 1), chunk_0)
        z_step(2 * i + 1, chunk_1)
        return 0

    lax.fori_loop(0, steps // 2, two_steps, 0, unroll=4)

    def y_step(c, _):
        high, low = split(rows_z[c])
        result = jnp.dot(y_table[...], jnp.concatenate([high, low, high], 0), preferred_element_type=F32)
        for part in range(2):
            for xh in range(2):
                block = result[part * length : (part + 1) * length, xh * LANES : (xh + 1) * LANES]
                plane[pl.ds(c * (4 * length) + part * 2 + xh, length, stride=4), :] = block
        return 0

    lax.fori_loop(0, half, y_step, 0, unroll=33)


def transform(psi_v, psi_c, meta, pair_count, devices):
    planes, plane_size = psi_v.shape[1], psi_v.shape[2]
    length = math.isqrt(plane_size)
    half = length // 2 + 1
    vmem = pl.BlockSpec(memory_space=pltpu.VMEM)
    extra, width = meta.shape[0] - devices, meta.shape[2]
    index = jax.ShapeDtypeStruct((devices, 1, width), jnp.int32)
    return pl.pallas_call(
        functools.partial(transform_kernel, length, pair_count),
        out_shape=[
            jax.ShapeDtypeStruct((half * length * 4, LANES), F32),
            jax.ShapeDtypeStruct((2 * length, 4 * LANES), BF16),
            index,
            index,
        ],
        in_specs=[vmem, vmem, pl.BlockSpec(memory_space=pl.ANY)],
        out_specs=[vmem] * 4,
        scratch_shapes=[
            pltpu.VMEM(psi_v.shape, F32),
            pltpu.VMEM((pair_count, planes, plane_size), BF16),
            pltpu.VMEM(((half + half % 2) * 8, 6 * LANES), BF16),
            pltpu.VMEM((2 * length, 6 * length), BF16),
            pltpu.VMEM((2, pair_count * planes, LANES), F32),
            pltpu.VMEM((2, pair_count * planes, LANES), F32),
            pltpu.VMEM((half, 2 * length, 2 * LANES), F32),
            pltpu.SMEM((extra, 1, width), jnp.int32),
            pltpu.SemaphoreType.DMA((pair_count + 1,)),
        ],
        compiler_params=pltpu.CompilerParams(vmem_limit_bytes=40 * 2**20),
        name="transform",
    )(meta, psi_v, psi_c)


def landing(chip, chips):
    return chip * 2 % chips + chip // (chips // 2)


def points_kernel(length, pair_count, width, orders, spot, phase, plane, coef, pick, *refs):
    *refs, tiles_0, tiles_1, peak, local, sems = refs
    outs = refs[-max(len(orders), 1) :]
    me = lax.axis_index("fft")
    blocks, rows = outs[0].shape[0], outs[0].shape[1]
    last = blocks * len(outs) - 1
    chunked = len(orders) > 0
    which = lax.broadcasted_iota(jnp.int32, (2 * length, width), 0) % length

    def index_of(block):
        if not chunked:
            return block
        group, block = block // blocks, block % blocks
        far, across = (
            sum(jnp.where(group == k, order[axis], 0) for k, order in enumerate(orders)) for axis in range(2)
        )
        half = lax.rem(lax.rem(me, 2) + far, 2)
        chips = phase.shape[0] // 2
        return half * chips + landing(jnp.bitwise_xor(me // 2, 2 * block + across), chips)

    def fetch(block):
        return pltpu.make_async_copy(spot.at[index_of(block)], local.at[block], sems.at[block])

    def gather(block, tiles):
        for start in range(0, width, UNROLL):
            loaded = [plane[local[block, 0, start + u]] for u in range(UNROLL)]
            for u in range(UNROLL):
                tiles[(start + u) * 4 : (start + u + 1) * 4, :] = loaded[u]

    def combine(group, block, tiles):
        out = outs[group]
        turns = phase[index_of(group * blocks + block)]
        one_hot = jnp.where(which == turns % length, 1.0, 0.0).astype(BF16)
        factors = lax.dot_general(
            one_hot, coef[...], (((0,), (0,)), ((), ())), preferred_element_type=F32
        )
        cos = [factors[:, k * LANES : (k + 1) * LANES] for k in range(2)]
        sin = [factors[:, (k + 2) * LANES : (k + 3) * LANES] for k in range(2)]
        real = [tiles[pl.ds(k, width, stride=4), :] for k in range(2)]
        imag = [tiles[pl.ds(k + 2, width, stride=4), :] for k in range(2)]
        sums = (
            cos[0] * real[0] + sin[0] * imag[0] + (cos[1] * real[1] + sin[1] * imag[1]),
            cos[0] * imag[0] - sin[0] * real[0] + (cos[1] * imag[1] - sin[1] * real[1]),
        )
        sign = jnp.where(turns >= length, -1.0, 1.0)
        for to_imag in range(2):
            high, low = split(sums[to_imag])
            result = dot_nt(pick[...], jnp.concatenate([high, low], 1))
            if to_imag:
                result = result * sign
            if not chunked:
                out[block, to_imag * pair_count : (to_imag + 1) * pair_count, :] = result
                continue
            for k in range(width // LANES):
                start = (2 * k + to_imag) * pair_count
                tile = result[:, k * LANES : (k + 1) * LANES]
                out[block, start : start + pair_count, :] = tile
                peak[...] = jnp.maximum(peak[...], jnp.abs(tile))

    for block in range(last + 1):
        fetch(block).start()
    peak[...] = jnp.zeros_like(peak)
    fetch(0).wait()
    gather(0, tiles_0)
    for block in range(1, last + 1):
        fetch(block).wait()
    for group in range(len(outs)):

        def two_blocks(step, _):
            block = group * blocks + 2 * step
            gather(block + 1, tiles_1)
            combine(group, 2 * step, tiles_0)
            gather(jnp.minimum(block + 2, last), tiles_0)
            combine(group, 2 * step + 1, tiles_1)
            return 0

        lax.fori_loop(0, blocks // 2, two_blocks, 0)
    if chunked:
        used = width // LANES * 2 * pair_count
        top = jnp.broadcast_to(jnp.max(peak[...], axis=0, keepdims=True), (rows - used, LANES))
        for out in outs:
            for block in range(blocks):
                out[block, used:, :] = top


def points(spot, phase, plane, coef, pick, pair_count, out_shape, orders, after):
    after = () if after is None else (after,)
    count = max(len(orders), 1)
    length, width = coef.shape[0] // 2, phase.shape[2]
    vmem = pl.BlockSpec(memory_space=pltpu.VMEM)
    hbm = pl.BlockSpec(memory_space=pl.ANY)
    return pl.pallas_call(
        functools.partial(points_kernel, length, pair_count, width, orders),
        out_shape=[jax.ShapeDtypeStruct(out_shape, F32)] * count,
        in_specs=[hbm] + [vmem] * 4 + [hbm] * len(after),
        out_specs=[vmem] * count,
        scratch_shapes=[
            pltpu.VMEM((width * 4, LANES), F32),
            pltpu.VMEM((width * 4, LANES), F32),
            pltpu.VMEM((pair_count, LANES), F32),
            pltpu.SMEM((count * out_shape[0], 1, width), jnp.int32),
            pltpu.SemaphoreType.DMA((count * out_shape[0],)),
        ],
        compiler_params=pltpu.CompilerParams(vmem_limit_bytes=12 * 2**20),
        cost_estimate=pl.CostEstimate(flops=10**8 * out_shape[0], bytes_accessed=2**20, transcendentals=0),
        name="points",
    )(spot, phase, plane, coef, pick, *after)


def sphere_parts(psi_v, psi_c, pair_v, pair_c, g_index, devices, paired):
    pair_count = pair_v.shape[0]
    width = g_index.shape[0] // devices
    filling = jnp.zeros(-(g_index.shape[0] + 2 * pair_count) % math.lcm(width, 1024), jnp.int32)
    meta = jnp.concatenate([g_index, pair_v, pair_c, filling]).reshape(-1, 1, width)
    plane, coef, spot, phase = transform(psi_v, psi_c, meta, pair_count, devices)
    pick = (np.arange(2 * LANES)[None, :] % SLOT == np.arange(pair_count)[:, None]).astype(jnp.bfloat16)
    rest = (spot, phase, plane.reshape(-1, 4, LANES), coef, pick, pair_count)
    if not paired:
        return points(*rest, (devices, 2 * pair_count, width), (), None)[0]
    shape = (devices // 4, width // LANES * 2 * pair_count + 8, LANES)
    return [functools.partial(points, *rest, shape, orders) for orders in (((1, 1),), ((0, 1),), ((1, 0), (0, 0)))]


def chi_kernel(groups, pair_count, first, rows, cols, real, imag, left):
    width = rows.shape[1]

    @pl.when(pl.program_id(0) == 0)
    def _():
        own = rows[...].astype(F32)
        cross = []
        for group in range(groups):
            start = group * 2 * pair_count
            cross.append(-own[start + pair_count : start + 2 * pair_count])
            cross.append(own[start : start + pair_count])
        left[:width] = (-own).T.astype(BF16)
        left[width:] = jnp.concatenate(cross, 0).T.astype(BF16)

    for k in range(cols.shape[0]):
        both = jnp.dot(left[...], cols[k], preferred_element_type=F32)
        real[:, k * width : (k + 1) * width] = both[:width]
        imag[:, k * width : (k + 1) * width] = both[width:]


def chi_blocks(rows, cols, first, blocks, groups, pair_count):
    depth, width = rows.shape
    out = jax.ShapeDtypeStruct((width, blocks * width), F32)
    step = LANES // math.gcd(width, LANES)
    out_spec = pl.BlockSpec((width, step * width), lambda j, first: (0, j))
    return pl.pallas_call(
        functools.partial(chi_kernel, groups, pair_count),
        out_shape=(out, out),
        grid_spec=pltpu.PrefetchScalarGridSpec(
            num_scalar_prefetch=1,
            grid=(blocks // step,),
            in_specs=[
                pl.BlockSpec((depth, width), lambda j, first: (0, 0)),
                pl.BlockSpec((step, depth, width), lambda j, first: (first[0] // step + j, 0, 0)),
            ],
            out_specs=(out_spec, out_spec),
            scratch_shapes=[pltpu.VMEM((2 * width, depth), BF16)],
        ),
        compiler_params=pltpu.CompilerParams(vmem_limit_bytes=32 * 2**20),
        name="chi",
    )(first, rows, cols)


def chi_direct_kernel(pair_count, width, shifts, has_left, *refs):
    depth = 2 * pair_count
    chunks = width // LANES
    wide = lambda piece: jnp.concatenate([piece[k * depth : (k + 1) * depth] for k in range(chunks)], 1)
    chip, chips = lax.axis_index("fft") // 2, lax.axis_size("fft") // 2
    if has_left:
        left, refs = refs[0], refs[3:]
        *cols, real, imag, stage, sems = refs
    else:
        row_refs, refs = refs[:2], refs[2:]
        *cols, real, imag, left, stage, sems = refs
        own = [wide(piece[...].astype(F32)) for piece in row_refs]
        cross = [part for piece in own for part in (-piece[pair_count:], piece[:pair_count])]
        left[:width] = (-jnp.concatenate(own, 0)).T.astype(BF16)
        left[width:] = jnp.concatenate(cross, 0).T.astype(BF16)

    def copies(s):
        block = landing(jnp.bitwise_xor(chip, shifts[s]), chips)
        start = pl.multiple_of(block * width, LANES)
        return [
            pltpu.make_async_copy(
                stage.at[s, pl.ds(i * width, width)], out.at[:, pl.ds(start, width)], sems.at[s, i]
            )
            for i, out in enumerate((real, imag))
        ]

    s = 0
    for own_pairs, other_pairs in zip(cols[::2], cols[1::2]):
        for start in range(0, own_pairs.shape[0], 2):
            rights = [
                jnp.concatenate([wide(own_pairs[k]), wide(other_pairs[k])], 0) for k in (start, start + 1)
            ]
            both = jnp.dot(left[...], jnp.concatenate(rights, 1), preferred_element_type=F32)
            for k in range(2):
                stage[s + k] = both[:, k * width : (k + 1) * width]
                for copy in copies(s + k):
                    copy.start()
            s += 2
    for s in range(len(shifts)):
        for copy in copies(s):
            copy.wait()


def chi_direct(rows, cols, shifts, done, pair_count, width, blocks):
    out = jax.ShapeDtypeStruct((width, blocks * width), F32)
    left = jax.ShapeDtypeStruct((2 * width, 4 * pair_count), BF16)
    vmem = pl.BlockSpec(memory_space=pltpu.VMEM)
    hbm = pl.BlockSpec(memory_space=pl.ANY)
    if done is None:
        args, specs, aliases = rows, [vmem, vmem], {}
        out_shape, out_specs = (out, out, left), (hbm, hbm, vmem)
    else:
        real, imag, left = done
        args, specs, aliases = (left, real, imag), [vmem, hbm, hbm], {1: 0, 2: 1}
        out_shape, out_specs = (out, out), (hbm, hbm)
    cols = [array for pair in cols for array in pair]
    count = len(shifts)
    return pl.pallas_call(
        functools.partial(chi_direct_kernel, pair_count, width, shifts, done is not None),
        out_shape=out_shape,
        in_specs=specs + [vmem] * len(cols),
        out_specs=out_specs,
        scratch_shapes=[
            pltpu.VMEM((count, 2 * width, width), F32),
            pltpu.SemaphoreType.DMA((count, 2)),
        ],
        input_output_aliases=aliases,
        compiler_params=pltpu.CompilerParams(vmem_limit_bytes=32 * 2**20),
        cost_estimate=pl.CostEstimate(flops=1, bytes_accessed=1, transcendentals=0),
        name="chi",
    )(*args, *cols)


def pair_factor(energy_v, energy_c, pair_v, pair_c, length):
    chosen = lambda table, which: jnp.sum(
        jnp.where(which[:, None] == jnp.arange(table.shape[0])[None, :], table[None, :], 0.0), 1
    )
    weight = 2.0 / (chosen(energy_c, pair_c) - chosen(energy_v, pair_v))
    return jnp.sqrt(weight) * (pair_v.shape[0] * lax.axis_size("grp")) ** (-0.25) * length ** (-1.5)


def permute(values, moves):
    chips = lax.axis_size("fft") // 2
    perm = []
    for chip in range(chips):
        for core in range(2):
            for y in range(2):
                to_chip, to_core, to_y = moves(chip, core, y)
                perm.append((chip * 4 + core * 2 + y, to_chip * 4 + to_core * 2 + to_y))
    return lax.ppermute(values, ("fft", "grp"), perm)


def encode(values, used):
    top = values[..., used : used + 1, :]
    exponent = jnp.ceil(jnp.log2(jnp.maximum(top, 2.0**-100))) - 14.0
    row = lax.broadcasted_iota(jnp.int32, values.shape, values.ndim - 2)
    return jnp.where(row < used, values * jnp.exp2(-exponent), exponent).astype(jnp.float16)


def decode(coded, used):
    scale = jnp.exp2(coded[..., used : used + 1, :].astype(F32))
    row = lax.broadcasted_iota(jnp.int32, coded.shape, coded.ndim - 2)
    return jnp.where(row < used, coded.astype(F32), 2.0**14) * scale


def two_groups(psi_v, psi_c, energy_v, energy_c, pair_v, pair_c, g_index):
    devices = lax.axis_size("fft")
    chips = devices // 2
    quarter = chips // 2
    length = math.isqrt(psi_v.shape[2])
    pair_count = pair_v.shape[0]
    width = g_index.shape[0] // devices
    chunks = width // LANES
    used = chunks * 2 * pair_count
    fft, grp = lax.axis_index("fft"), lax.axis_index("grp")
    swap = lambda values: permute(values, lambda chip, core, y: (chip, 1 - core, y))
    swap_x = lambda values: permute(values, lambda chip, core, y: (chip ^ 1, core, y))

    calls = sphere_parts(psi_v, psi_c, pair_v, pair_c, g_index, devices, True)
    (far,) = calls[0](None)
    arrived = swap(far)
    (across,) = calls[1](far)
    across = across + arrived
    coded, across = lax.optimization_barrier((encode(across, used), across))
    arrived_x = swap_x(coded)
    far, kept = calls[2](across)
    arrived_x, far = lax.optimization_barrier((arrived_x, far))
    kept = kept + swap(far) + decode(arrived_x, used)
    (pair_v, pair_c), kept = lax.optimization_barrier(((pair_v, pair_c), kept))
    factor = pair_factor(energy_v, energy_c, pair_v, pair_c, length)
    factor = jnp.tile(factor, 2 * chunks)[:, None]
    total = kept[0]
    for s in reversed(range(1, quarter)):
        move = lambda chip, core, y, s=s: (chip ^ (2 * s), core, y)
        total = total + decode(permute(encode(kept[s], used), move), used)
    own = (total[:used] * factor).astype(BF16)

    first = jnp.stack(
        [permute(own, lambda chip, core, y, s=s: (chip ^ (2 * s), y, core)) for s in range(quarter)]
    )
    first = lax.optimization_barrier(first)
    first_x = swap_x(first)
    halves = [first[: quarter // 2], first[quarter // 2 :]]
    second = [swap(half) for half in halves]

    def row_home(chip, core):
        return chip % quarter + core * quarter, chip // quarter

    same = permute(own, lambda chip, core, y: (*row_home(chip, core), y))
    cross = permute(own, lambda chip, core, y: (*row_home(chip, core), 1 - y))
    agree = fft % 2 == grp
    rows = (jnp.where(agree, same, cross), jnp.where(agree, cross, same))
    shifts = [2 * s for s in range(quarter)]
    real, imag, left = chi_direct(rows, list(zip(halves, second)), shifts, None, pair_count, width, chips)
    first_x, left = lax.optimization_barrier((first_x, left))
    shifts = [2 * s + 1 for s in range(quarter)]
    return chi_direct(None, [(first_x, swap(first_x))], shifts, (real, imag, left), pair_count, width, chips)


def any_groups(psi_v, psi_c, energy_v, energy_c, pair_v, pair_c, g_index):
    devices, groups = lax.axis_size("fft"), lax.axis_size("grp")
    length = math.isqrt(psi_v.shape[2])
    pair_count = pair_v.shape[0]
    parts = sphere_parts(psi_v, psi_c, pair_v, pair_c, g_index, devices, False)
    factor = pair_factor(energy_v, energy_c, pair_v, pair_c, length)
    factor = jnp.concatenate([factor, factor])
    arrived = lax.all_to_all(parts, "fft", split_axis=0, concat_axis=0, tiled=True)
    own = (jnp.sum(arrived, 0) * factor[:, None]).astype(BF16)
    rows = lax.all_gather(own, "grp", axis=0, tiled=True)
    cols = lax.all_gather(rows, "fft", axis=0, tiled=False)
    blocks = devices // groups
    first = (lax.axis_index("grp") * blocks).astype(jnp.int32).reshape(1)
    return chi_blocks(rows, cols, first, blocks, groups, pair_count)


def per_device(
    psi_valence,
    psi_conduction,
    energy_valence,
    energy_conduction,
    pair_valence,
    pair_conduction,
    g_index,
):
    args = (
        psi_valence,
        psi_conduction,
        energy_valence,
        energy_conduction,
        pair_valence,
        pair_conduction,
        g_index,
    )
    devices = lax.axis_size("fft")
    chips = devices // 2
    power_of_two = devices % 2 == 0 and chips & (chips - 1) == 0
    if lax.axis_size("grp") == 2 and power_of_two and chips >= 4 and g_index.shape[0] % (devices * LANES) == 0:
        return two_groups(*args)
    return any_groups(*args)


def solution(mesh):
    placed = (P(None, "fft", None), P(None, "fft", None), P(), P(), P("grp"), P("grp"), P())
    return jax.shard_map(
        per_device,
        mesh=mesh,
        in_specs=placed,
        out_specs=(P("fft", "grp"), P("fft", "grp")),
        check_vma=False,
    )
```

```python
import functools
import math

import jax
import jax.numpy as jnp
import numpy as np
from jax import lax
from jax.experimental import pallas as pl
from jax.experimental.pallas import tpu as pltpu
from jax.sharding import PartitionSpec as P

LANES = 128
SLOT = 64
UNROLL = 8
BF16 = jnp.bfloat16
F32 = jnp.float32


def cosine(turn, length):
    from_half = jnp.abs(turn - length // 2)
    folded = jnp.minimum(from_half, length // 2 - from_half)
    square = (folded.astype(F32) * (2.0 * math.pi / length)) ** 2
    value = jnp.full(square.shape, 1.0 / math.factorial(12), F32)
    for order in range(10, -1, -2):
        value = value * square + (-1.0) ** (order // 2) / math.factorial(order)
    return jnp.where(from_half > length // 4, value, -value)


def split(values):
    high = values.astype(BF16)
    low = (values - high.astype(F32)).astype(BF16)
    return high, low


def dot_nt(left, right):
    return lax.dot_general(left, right, (((1,), (1,)), ((), ())), preferred_element_type=F32)


def put(table, values):
    high, low = split(values)
    for k, part in enumerate((high, high, low)):
        table[:, k * values.shape[1] : (k + 1) * values.shape[1]] = part


def fill_z_table(length, z_table):
    quarter = length // 4
    group = 2 * LANES // length
    shape = (z_table.shape[0], group * length)
    row, column = (lax.broadcasted_iota(jnp.int32, shape, axis) for axis in range(2))
    c, to_imag, y = row // (2 * group), row // group % 2, row % group
    value = cosine((c * (column % length) + quarter * to_imag) % length, length)
    put(z_table, jnp.where(column // length == y, value, 0.0))


def fill_tables(length, planes, y_table, coef):
    quarter = length // 4
    group = 2 * LANES // length
    shape = (2 * length, 2 * length)
    row, column = (lax.broadcasted_iota(jnp.int32, shape, axis) for axis in range(2))
    y, from_imag = column // (2 * group) * group + column % group, column // group % 2
    turn = row % length * y + quarter * (row // length - from_imag) + length
    put(y_table, cosine(turn % length, length))
    shape = (length, 4 * LANES)
    a, lane = (lax.broadcasted_iota(jnp.int32, shape, axis) for axis in range(2))
    x = lax.axis_index("fft") * planes + lane % (2 * LANES) // SLOT
    turn = a * x - quarter * (lane // (2 * LANES)) + length
    high, low = split(cosine(turn % length, length))
    coef[:length] = high
    coef[length:] = low


def transform_kernel(length, pair_count, meta, psi_v, psi_c, plane, coef, spot, phase, *scratch):
    val, con, z_table, y_table, chunk_0, chunk_1, rows_z, pairs, sems = scratch
    width, count = meta.shape[2], spot.shape[0]
    pairs_copy = pltpu.make_async_copy(meta.at[pl.ds(count, pairs.shape[0])], pairs, sems.at[pair_count])
    pairs_copy.start()
    fill_z_table(length, z_table)
    pairs_copy.wait()
    valence = [pairs[p // width, 0, p % width] for p in range(pair_count)]
    conduction = [pairs[p // width, 0, p % width] for p in range(pair_count, 2 * pair_count)]
    half = length // 2 + 1
    planes = psi_v.shape[1]
    steps = psi_v.shape[2] // (2 * LANES)

    def pair_copy(p):
        return pltpu.make_async_copy(psi_c.at[conduction[p]], con.at[p], sems.at[p])

    for p in range(pair_count):
        pair_copy(p).start()
    fill_tables(length, planes, y_table, coef)
    points = meta[:count]
    a, b, c = points // (length * length), points // length % length, points % length
    flip = c > length // 2
    mirrored = lambda k: jnp.where(flip, (length - k) % length, k)
    spot[...] = mirrored(c) * length + mirrored(b)
    phase[...] = mirrored(a) + jnp.where(flip, length, 0)
    val[...] = psi_v[...].astype(F32)
    for p in range(pair_count):
        pair_copy(p).wait()

    def density(step, chunk):
        lanes = pl.ds(pl.multiple_of(step * (2 * LANES), 2 * LANES), 2 * LANES)
        for p in range(pair_count):
            values = con[p, :, lanes].astype(F32) * val[valence[p], :, lanes]
            for k in range(2):
                chunk[k, p * planes : (p + 1) * planes, :] = values[:, k * LANES : (k + 1) * LANES]

    def z_step(step, chunk):
        parts = []
        for k in range(2):
            blocks = []
            for x in range(planes):
                blocks.append(chunk[k, pl.ds(x, pair_count, stride=planes), :])
                blocks.append(jnp.zeros((SLOT - pair_count, LANES), F32))
            blocks += [jnp.zeros((SLOT, LANES), F32)] * (4 - planes)
            parts.append(jnp.concatenate(blocks, 0))
        high, low = split(jnp.concatenate(parts, 1))
        result = dot_nt(z_table[...], jnp.concatenate([high, low, high], 1))[: half * 8]
        rows_z[:, pl.ds(pl.multiple_of(step * 8, 8), 8), :] = result.reshape(half, 8, 2 * LANES)

    density(0, chunk_0)

    def two_steps(i, _):
        density(2 * i + 1, chunk_1)
        z_step(2 * i, chunk_0)
        density(jnp.minimum(2 * i + 2, steps - 1), chunk_0)
        z_step(2 * i + 1, chunk_1)
        return 0

    lax.fori_loop(0, steps // 2, two_steps, 0, unroll=8)

    def y_step(c, _):
        high, low = split(rows_z[c])
        result = jnp.dot(y_table[...], jnp.concatenate([high, low, high], 0), preferred_element_type=F32)
        for part in range(2):
            for xh in range(2):
                block = result[part * length : (part + 1) * length, xh * LANES : (xh + 1) * LANES]
                plane[pl.ds(c * (4 * length) + part * 2 + xh, length, stride=4), :] = block
        return 0

    lax.fori_loop(0, half, y_step, 0, unroll=33)


def transform(psi_v, psi_c, meta, pair_count, devices):
    planes, plane_size = psi_v.shape[1], psi_v.shape[2]
    length = math.isqrt(plane_size)
    half = length // 2 + 1
    vmem = pl.BlockSpec(memory_space=pltpu.VMEM)
    extra, width = meta.shape[0] - devices, meta.shape[2]
    index = jax.ShapeDtypeStruct((devices, 1, width), jnp.int32)
    return pl.pallas_call(
        functools.partial(transform_kernel, length, pair_count),
        out_shape=[
            jax.ShapeDtypeStruct((half * length * 4, LANES), F32),
            jax.ShapeDtypeStruct((2 * length, 4 * LANES), BF16),
            index,
            index,
        ],
        in_specs=[vmem, vmem, pl.BlockSpec(memory_space=pl.ANY)],
        out_specs=[vmem] * 4,
        scratch_shapes=[
            pltpu.VMEM(psi_v.shape, F32),
            pltpu.VMEM((pair_count, planes, plane_size), BF16),
            pltpu.VMEM(((half + half % 2) * 8, 6 * LANES), BF16),
            pltpu.VMEM((2 * length, 6 * length), BF16),
            pltpu.VMEM((2, pair_count * planes, LANES), F32),
            pltpu.VMEM((2, pair_count * planes, LANES), F32),
            pltpu.VMEM((half, 2 * length, 2 * LANES), F32),
            pltpu.SMEM((extra, 1, width), jnp.int32),
            pltpu.SemaphoreType.DMA((pair_count + 1,)),
        ],
        compiler_params=pltpu.CompilerParams(vmem_limit_bytes=40 * 2**20),
        name="transform",
    )(meta, psi_v, psi_c)


def landing(chip, chips):
    return chip * 2 % chips + chip // (chips // 2)


def points_kernel(length, pair_count, width, orders, spot, phase, plane, coef, pick, *refs):
    *refs, tiles_0, tiles_1, peak, local, sems = refs
    outs = refs[-max(len(orders), 1) :]
    me = lax.axis_index("fft")
    blocks, rows = outs[0].shape[0], outs[0].shape[1]
    last = blocks * len(outs) - 1
    chunked = len(orders) > 0
    which = lax.broadcasted_iota(jnp.int32, (2 * length, width), 0) % length

    def index_of(block):
        if not chunked:
            return block
        group, block = block // blocks, block % blocks
        far, across = (
            sum(jnp.where(group == k, order[axis], 0) for k, order in enumerate(orders)) for axis in range(2)
        )
        half = lax.rem(lax.rem(me, 2) + far, 2)
        chips = phase.shape[0] // 2
        return half * chips + landing(jnp.bitwise_xor(me // 2, 2 * block + across), chips)

    def fetch(block):
        return pltpu.make_async_copy(spot.at[index_of(block)], local.at[block], sems.at[block])

    def gather(block, tiles):
        for start in range(0, width, UNROLL):
            loaded = [plane[local[block, 0, start + u]] for u in range(UNROLL)]
            for u in range(UNROLL):
                tiles[(start + u) * 4 : (start + u + 1) * 4, :] = loaded[u]

    def combine(group, block, tiles):
        out = outs[group]
        turns = phase[index_of(group * blocks + block)]
        one_hot = jnp.where(which == turns % length, 1.0, 0.0).astype(BF16)
        factors = lax.dot_general(
            one_hot, coef[...], (((0,), (0,)), ((), ())), preferred_element_type=F32
        )
        cos = [factors[:, k * LANES : (k + 1) * LANES] for k in range(2)]
        sin = [factors[:, (k + 2) * LANES : (k + 3) * LANES] for k in range(2)]
        real = [tiles[pl.ds(k, width, stride=4), :] for k in range(2)]
        imag = [tiles[pl.ds(k + 2, width, stride=4), :] for k in range(2)]
        sums = (
            cos[0] * real[0] + sin[0] * imag[0] + (cos[1] * real[1] + sin[1] * imag[1]),
            cos[0] * imag[0] - sin[0] * real[0] + (cos[1] * imag[1] - sin[1] * real[1]),
        )
        sign = jnp.where(turns >= length, -1.0, 1.0)
        for to_imag in range(2):
            high, low = split(sums[to_imag])
            result = dot_nt(pick[...], jnp.concatenate([high, low], 1))
            if to_imag:
                result = result * sign
            if not chunked:
                out[block, to_imag * pair_count : (to_imag + 1) * pair_count, :] = result
                continue
            for k in range(width // LANES):
                start = (2 * k + to_imag) * pair_count
                tile = result[:, k * LANES : (k + 1) * LANES]
                out[block, start : start + pair_count, :] = tile
                peak[...] = jnp.maximum(peak[...], jnp.abs(tile))

    for block in range(last + 1):
        fetch(block).start()
    peak[...] = jnp.zeros_like(peak)
    fetch(0).wait()
    gather(0, tiles_0)
    for block in range(1, last + 1):
        fetch(block).wait()
    for group in range(len(outs)):

        def two_blocks(step, _):
            block = group * blocks + 2 * step
            gather(block + 1, tiles_1)
            combine(group, 2 * step, tiles_0)
            gather(jnp.minimum(block + 2, last), tiles_0)
            combine(group, 2 * step + 1, tiles_1)
            return 0

        lax.fori_loop(0, blocks // 2, two_blocks, 0, unroll=2)
    if chunked:
        used = width // LANES * 2 * pair_count
        top = jnp.broadcast_to(jnp.max(peak[...], axis=0, keepdims=True), (rows - used, LANES))
        for out in outs:
            for block in range(blocks):
                out[block, used:, :] = top


def points(spot, phase, plane, coef, pick, pair_count, out_shape, orders, after):
    after = () if after is None else (after,)
    count = max(len(orders), 1)
    length, width = coef.shape[0] // 2, phase.shape[2]
    vmem = pl.BlockSpec(memory_space=pltpu.VMEM)
    hbm = pl.BlockSpec(memory_space=pl.ANY)
    return pl.pallas_call(
        functools.partial(points_kernel, length, pair_count, width, orders),
        out_shape=[jax.ShapeDtypeStruct(out_shape, F32)] * count,
        in_specs=[hbm] + [vmem] * 4 + [hbm] * len(after),
        out_specs=[vmem] * count,
        scratch_shapes=[
            pltpu.VMEM((width * 4, LANES), F32),
            pltpu.VMEM((width * 4, LANES), F32),
            pltpu.VMEM((pair_count, LANES), F32),
            pltpu.SMEM((count * out_shape[0], 1, width), jnp.int32),
            pltpu.SemaphoreType.DMA((count * out_shape[0],)),
        ],
        compiler_params=pltpu.CompilerParams(vmem_limit_bytes=12 * 2**20),
        cost_estimate=pl.CostEstimate(flops=10**8 * out_shape[0], bytes_accessed=2**20, transcendentals=0),
        name="points",
    )(spot, phase, plane, coef, pick, *after)


def sphere_parts(psi_v, psi_c, pair_v, pair_c, g_index, devices, paired):
    pair_count = pair_v.shape[0]
    width = g_index.shape[0] // devices
    filling = jnp.zeros(-(g_index.shape[0] + 2 * pair_count) % math.lcm(width, 1024), jnp.int32)
    meta = jnp.concatenate([g_index, pair_v, pair_c, filling]).reshape(-1, 1, width)
    plane, coef, spot, phase = transform(psi_v, psi_c, meta, pair_count, devices)
    pick = (np.arange(2 * LANES)[None, :] % SLOT == np.arange(pair_count)[:, None]).astype(jnp.bfloat16)
    rest = (spot, phase, plane.reshape(-1, 4, LANES), coef, pick, pair_count)
    if not paired:
        return points(*rest, (devices, 2 * pair_count, width), (), None)[0]
    shape = (devices // 4, width // LANES * 2 * pair_count + 8, LANES)
    return [functools.partial(points, *rest, shape, orders) for orders in (((1, 1),), ((0, 1),), ((1, 0), (0, 0)))]


def chi_kernel(groups, pair_count, first, rows, cols, real, imag, left):
    width = rows.shape[1]

    @pl.when(pl.program_id(0) == 0)
    def _():
        own = rows[...].astype(F32)
        cross = []
        for group in range(groups):
            start = group * 2 * pair_count
            cross.append(-own[start + pair_count : start + 2 * pair_count])
            cross.append(own[start : start + pair_count])
        left[:width] = (-own).T.astype(BF16)
        left[width:] = jnp.concatenate(cross, 0).T.astype(BF16)

    for k in range(cols.shape[0]):
        both = jnp.dot(left[...], cols[k], preferred_element_type=F32)
        real[:, k * width : (k + 1) * width] = both[:width]
        imag[:, k * width : (k + 1) * width] = both[width:]


def chi_blocks(rows, cols, first, blocks, groups, pair_count):
    depth, width = rows.shape
    out = jax.ShapeDtypeStruct((width, blocks * width), F32)
    step = LANES // math.gcd(width, LANES)
    out_spec = pl.BlockSpec((width, step * width), lambda j, first: (0, j))
    return pl.pallas_call(
        functools.partial(chi_kernel, groups, pair_count),
        out_shape=(out, out),
        grid_spec=pltpu.PrefetchScalarGridSpec(
            num_scalar_prefetch=1,
            grid=(blocks // step,),
            in_specs=[
                pl.BlockSpec((depth, width), lambda j, first: (0, 0)),
                pl.BlockSpec((step, depth, width), lambda j, first: (first[0] // step + j, 0, 0)),
            ],
            out_specs=(out_spec, out_spec),
            scratch_shapes=[pltpu.VMEM((2 * width, depth), BF16)],
        ),
        compiler_params=pltpu.CompilerParams(vmem_limit_bytes=32 * 2**20),
        name="chi",
    )(first, rows, cols)


def chi_direct_kernel(pair_count, width, shifts, has_left, *refs):
    depth = 2 * pair_count
    chunks = width // LANES
    wide = lambda piece: jnp.concatenate([piece[k * depth : (k + 1) * depth] for k in range(chunks)], 1)
    chip, chips = lax.axis_index("fft") // 2, lax.axis_size("fft") // 2
    if has_left:
        left, refs = refs[0], refs[3:]
        *cols, real, imag, stage, sems = refs
    else:
        row_refs, refs = refs[:2], refs[2:]
        *cols, real, imag, left, stage, sems = refs
        own = [wide(piece[...].astype(F32)) for piece in row_refs]
        cross = [part for piece in own for part in (-piece[pair_count:], piece[:pair_count])]
        left[:width] = (-jnp.concatenate(own, 0)).T.astype(BF16)
        left[width:] = jnp.concatenate(cross, 0).T.astype(BF16)

    def copies(s):
        block = landing(jnp.bitwise_xor(chip, shifts[s]), chips)
        start = pl.multiple_of(block * width, LANES)
        return [
            pltpu.make_async_copy(
                stage.at[s, pl.ds(i * width, width)], out.at[:, pl.ds(start, width)], sems.at[s, i]
            )
            for i, out in enumerate((real, imag))
        ]

    s = 0
    for own_pairs, other_pairs in zip(cols[::2], cols[1::2]):
        for start in range(0, own_pairs.shape[0], 2):
            rights = [
                jnp.concatenate([wide(own_pairs[k]), wide(other_pairs[k])], 0) for k in (start, start + 1)
            ]
            both = jnp.dot(left[...], jnp.concatenate(rights, 1), preferred_element_type=F32)
            for k in range(2):
                stage[s + k] = both[:, k * width : (k + 1) * width]
                for copy in copies(s + k):
                    copy.start()
            s += 2
    for s in range(len(shifts)):
        for copy in copies(s):
            copy.wait()


def chi_direct(rows, cols, shifts, done, pair_count, width, blocks):
    out = jax.ShapeDtypeStruct((width, blocks * width), F32)
    left = jax.ShapeDtypeStruct((2 * width, 4 * pair_count), BF16)
    vmem = pl.BlockSpec(memory_space=pltpu.VMEM)
    hbm = pl.BlockSpec(memory_space=pl.ANY)
    if done is None:
        args, specs, aliases = rows, [vmem, vmem], {}
        out_shape, out_specs = (out, out, left), (hbm, hbm, vmem)
    else:
        real, imag, left = done
        args, specs, aliases = (left, real, imag), [vmem, hbm, hbm], {1: 0, 2: 1}
        out_shape, out_specs = (out, out), (hbm, hbm)
    cols = [array for pair in cols for array in pair]
    count = len(shifts)
    return pl.pallas_call(
        functools.partial(chi_direct_kernel, pair_count, width, shifts, done is not None),
        out_shape=out_shape,
        in_specs=specs + [vmem] * len(cols),
        out_specs=out_specs,
        scratch_shapes=[
            pltpu.VMEM((count, 2 * width, width), F32),
            pltpu.SemaphoreType.DMA((count, 2)),
        ],
        input_output_aliases=aliases,
        compiler_params=pltpu.CompilerParams(vmem_limit_bytes=32 * 2**20),
        cost_estimate=pl.CostEstimate(flops=1, bytes_accessed=1, transcendentals=0),
        name="chi",
    )(*args, *cols)


def pair_factor(energy_v, energy_c, pair_v, pair_c, length):
    chosen = lambda table, which: jnp.sum(
        jnp.where(which[:, None] == jnp.arange(table.shape[0])[None, :], table[None, :], 0.0), 1
    )
    weight = 2.0 / (chosen(energy_c, pair_c) - chosen(energy_v, pair_v))
    return jnp.sqrt(weight) * (pair_v.shape[0] * lax.axis_size("grp")) ** (-0.25) * length ** (-1.5)


def permute(values, moves):
    chips = lax.axis_size("fft") // 2
    perm = []
    for chip in range(chips):
        for core in range(2):
            for y in range(2):
                to_chip, to_core, to_y = moves(chip, core, y)
                perm.append((chip * 4 + core * 2 + y, to_chip * 4 + to_core * 2 + to_y))
    return lax.ppermute(values, ("fft", "grp"), perm)


def encode(values, used):
    top = values[..., used : used + 1, :]
    exponent = jnp.ceil(jnp.log2(jnp.maximum(top, 2.0**-100))) - 14.0
    row = lax.broadcasted_iota(jnp.int32, values.shape, values.ndim - 2)
    return jnp.where(row < used, values * jnp.exp2(-exponent), exponent).astype(jnp.float16)


def decode(coded, used):
    scale = jnp.exp2(coded[..., used : used + 1, :].astype(F32))
    row = lax.broadcasted_iota(jnp.int32, coded.shape, coded.ndim - 2)
    return jnp.where(row < used, coded.astype(F32), 2.0**14) * scale


def two_groups(psi_v, psi_c, energy_v, energy_c, pair_v, pair_c, g_index):
    devices = lax.axis_size("fft")
    chips = devices // 2
    quarter = chips // 2
    length = math.isqrt(psi_v.shape[2])
    pair_count = pair_v.shape[0]
    width = g_index.shape[0] // devices
    chunks = width // LANES
    used = chunks * 2 * pair_count
    fft, grp = lax.axis_index("fft"), lax.axis_index("grp")
    swap = lambda values: permute(values, lambda chip, core, y: (chip, 1 - core, y))
    swap_x = lambda values: permute(values, lambda chip, core, y: (chip ^ 1, core, y))

    calls = sphere_parts(psi_v, psi_c, pair_v, pair_c, g_index, devices, True)
    (far,) = calls[0](None)
    arrived = swap(far)
    (across,) = calls[1](far)
    across = across + arrived
    coded, across = lax.optimization_barrier((encode(across, used), across))
    arrived_x = swap_x(coded)
    far, kept = calls[2](across)
    arrived_x, far = lax.optimization_barrier((arrived_x, far))
    kept = kept + swap(far) + decode(arrived_x, used)
    (pair_v, pair_c), kept = lax.optimization_barrier(((pair_v, pair_c), kept))
    factor = pair_factor(energy_v, energy_c, pair_v, pair_c, length)
    factor = jnp.tile(factor, 2 * chunks)[:, None]
    total = kept[0]
    for s in reversed(range(1, quarter)):
        move = lambda chip, core, y, s=s: (chip ^ (2 * s), core, y)
        total = total + decode(permute(encode(kept[s], used), move), used)
    own = (total[:used] * factor).astype(BF16)

    first = jnp.stack(
        [permute(own, lambda chip, core, y, s=s: (chip ^ (2 * s), y, core)) for s in range(quarter)]
    )
    first = lax.optimization_barrier(first)
    first_x = swap_x(first)
    halves = [first[: quarter // 2], first[quarter // 2 :]]
    second = [swap(half) for half in halves]

    def row_home(chip, core):
        return chip % quarter + core * quarter, chip // quarter

    same = permute(own, lambda chip, core, y: (*row_home(chip, core), y))
    cross = permute(own, lambda chip, core, y: (*row_home(chip, core), 1 - y))
    agree = fft % 2 == grp
    rows = (jnp.where(agree, same, cross), jnp.where(agree, cross, same))
    shifts = [2 * s for s in range(quarter)]
    real, imag, left = chi_direct(rows, list(zip(halves, second)), shifts, None, pair_count, width, chips)
    first_x, left = lax.optimization_barrier((first_x, left))
    shifts = [2 * s + 1 for s in range(quarter)]
    return chi_direct(None, [(first_x, swap(first_x))], shifts, (real, imag, left), pair_count, width, chips)


def any_groups(psi_v, psi_c, energy_v, energy_c, pair_v, pair_c, g_index):
    devices, groups = lax.axis_size("fft"), lax.axis_size("grp")
    length = math.isqrt(psi_v.shape[2])
    pair_count = pair_v.shape[0]
    parts = sphere_parts(psi_v, psi_c, pair_v, pair_c, g_index, devices, False)
    factor = pair_factor(energy_v, energy_c, pair_v, pair_c, length)
    factor = jnp.concatenate([factor, factor])
    arrived = lax.all_to_all(parts, "fft", split_axis=0, concat_axis=0, tiled=True)
    own = (jnp.sum(arrived, 0) * factor[:, None]).astype(BF16)
    rows = lax.all_gather(own, "grp", axis=0, tiled=True)
    cols = lax.all_gather(rows, "fft", axis=0, tiled=False)
    blocks = devices // groups
    first = (lax.axis_index("grp") * blocks).astype(jnp.int32).reshape(1)
    return chi_blocks(rows, cols, first, blocks, groups, pair_count)


def per_device(
    psi_valence,
    psi_conduction,
    energy_valence,
    energy_conduction,
    pair_valence,
    pair_conduction,
    g_index,
):
    args = (
        psi_valence,
        psi_conduction,
        energy_valence,
        energy_conduction,
        pair_valence,
        pair_conduction,
        g_index,
    )
    devices = lax.axis_size("fft")
    chips = devices // 2
    power_of_two = devices % 2 == 0 and chips & (chips - 1) == 0
    if lax.axis_size("grp") == 2 and power_of_two and chips >= 4 and g_index.shape[0] % (devices * LANES) == 0:
        return two_groups(*args)
    return any_groups(*args)


def solution(mesh):
    placed = (P(None, "fft", None), P(None, "fft", None), P(), P(), P("grp"), P("grp"), P())
    return jax.shard_map(
        per_device,
        mesh=mesh,
        in_specs=placed,
        out_specs=(P("fft", "grp"), P("fft", "grp")),
        check_vma=False,
    )
```

```python
import functools
import math

import jax
import jax.numpy as jnp
import numpy as np
from jax import lax
from jax.experimental import pallas as pl
from jax.experimental.pallas import tpu as pltpu
from jax.sharding import PartitionSpec as P

LANES = 128
SLOT = 64
UNROLL = 8
BF16 = jnp.bfloat16
F32 = jnp.float32


def cosine(turn, length):
    from_half = jnp.abs(turn - length // 2)
    folded = jnp.minimum(from_half, length // 2 - from_half)
    square = (folded.astype(F32) * (2.0 * math.pi / length)) ** 2
    value = jnp.full(square.shape, 1.0 / math.factorial(12), F32)
    for order in range(10, -1, -2):
        value = value * square + (-1.0) ** (order // 2) / math.factorial(order)
    return jnp.where(from_half > length // 4, value, -value)


def split(values):
    high = values.astype(BF16)
    low = (values - high.astype(F32)).astype(BF16)
    return high, low


def dot_nt(left, right):
    return lax.dot_general(left, right, (((1,), (1,)), ((), ())), preferred_element_type=F32)


def put(table, values):
    high, low = split(values)
    for k, part in enumerate((high, high, low)):
        table[:, k * values.shape[1] : (k + 1) * values.shape[1]] = part


def fill_z_table(length, z_table):
    quarter = length // 4
    group = 2 * LANES // length
    shape = (z_table.shape[0], group * length)
    row, column = (lax.broadcasted_iota(jnp.int32, shape, axis) for axis in range(2))
    c, to_imag, y = row // (2 * group), row // group % 2, row % group
    value = cosine((c * (column % length) + quarter * to_imag) % length, length)
    put(z_table, jnp.where(column // length == y, value, 0.0))


def fill_tables(length, planes, y_table, coef):
    quarter = length // 4
    group = 2 * LANES // length
    shape = (2 * length, 2 * length)
    row, column = (lax.broadcasted_iota(jnp.int32, shape, axis) for axis in range(2))
    y, from_imag = column // (2 * group) * group + column % group, column // group % 2
    turn = row % length * y + quarter * (row // length - from_imag) + length
    put(y_table, cosine(turn % length, length))
    shape = (length, 4 * LANES)
    a, lane = (lax.broadcasted_iota(jnp.int32, shape, axis) for axis in range(2))
    x = lax.axis_index("fft") * planes + lane % (2 * LANES) // SLOT
    turn = a * x - quarter * (lane // (2 * LANES)) + length
    high, low = split(cosine(turn % length, length))
    coef[:length] = high
    coef[length:] = low


def transform_kernel(length, pair_count, meta, psi_v, psi_c, plane, coef, spot, phase, *scratch):
    val, con, z_table, y_table, chunk_0, chunk_1, rows_z, pairs, sems = scratch
    width, count = meta.shape[2], spot.shape[0]
    pairs_copy = pltpu.make_async_copy(meta.at[pl.ds(count, pairs.shape[0])], pairs, sems.at[pair_count])
    pairs_copy.start()
    fill_z_table(length, z_table)
    pairs_copy.wait()
    valence = [pairs[p // width, 0, p % width] for p in range(pair_count)]
    conduction = [pairs[p // width, 0, p % width] for p in range(pair_count, 2 * pair_count)]
    half = length // 2 + 1
    planes = psi_v.shape[1]
    steps = psi_v.shape[2] // (2 * LANES)

    def pair_copy(p):
        return pltpu.make_async_copy(psi_c.at[conduction[p]], con.at[p], sems.at[p])

    for p in range(pair_count):
        pair_copy(p).start()
    fill_tables(length, planes, y_table, coef)
    points = meta[:count]
    a, b, c = points // (length * length), points // length % length, points % length
    flip = c > length // 2
    mirrored = lambda k: jnp.where(flip, (length - k) % length, k)
    spot[...] = mirrored(c) * length + mirrored(b)
    phase[...] = mirrored(a) + jnp.where(flip, length, 0)
    val[...] = psi_v[...].astype(F32)
    for p in range(pair_count):
        pair_copy(p).wait()

    def density(step, chunk):
        lanes = pl.ds(pl.multiple_of(step * (2 * LANES), 2 * LANES), 2 * LANES)
        for p in range(pair_count):
            values = con[p, :, lanes].astype(F32) * val[valence[p], :, lanes]
            for k in range(2):
                chunk[k, p * planes : (p + 1) * planes, :] = values[:, k * LANES : (k + 1) * LANES]

    def z_step(step, chunk):
        parts = []
        for k in range(2):
            blocks = []
            for x in range(planes):
                blocks.append(chunk[k, pl.ds(x, pair_count, stride=planes), :])
                blocks.append(jnp.zeros((SLOT - pair_count, LANES), F32))
            blocks += [jnp.zeros((SLOT, LANES), F32)] * (4 - planes)
            parts.append(jnp.concatenate(blocks, 0))
        high, low = split(jnp.concatenate(parts, 1))
        result = dot_nt(z_table[...], jnp.concatenate([high, low, high], 1))[: half * 8]
        rows_z[:, pl.ds(pl.multiple_of(step * 8, 8), 8), :] = result.reshape(half, 8, 2 * LANES)

    density(0, chunk_0)

    def two_steps(i, _):
        density(2 * i + 1, chunk_1)
        z_step(2 * i, chunk_0)
        density(jnp.minimum(2 * i + 2, steps - 1), chunk_0)
        z_step(2 * i + 1, chunk_1)
        return 0

    lax.fori_loop(0, steps // 2, two_steps, 0, unroll=8)

    def y_step(c, _):
        high, low = split(rows_z[c])
        result = jnp.dot(y_table[...], jnp.concatenate([high, low, high], 0), preferred_element_type=F32)
        for part in range(2):
            for xh in range(2):
                block = result[part * length : (part + 1) * length, xh * LANES : (xh + 1) * LANES]
                plane[pl.ds(c * (4 * length) + part * 2 + xh, length, stride=4), :] = block
        return 0

    lax.fori_loop(0, half, y_step, 0, unroll=33)


def transform(psi_v, psi_c, meta, pair_count, devices):
    planes, plane_size = psi_v.shape[1], psi_v.shape[2]
    length = math.isqrt(plane_size)
    half = length // 2 + 1
    vmem = pl.BlockSpec(memory_space=pltpu.VMEM)
    extra, width = meta.shape[0] - devices, meta.shape[2]
    index = jax.ShapeDtypeStruct((devices, 1, width), jnp.int32)
    return pl.pallas_call(
        functools.partial(transform_kernel, length, pair_count),
        out_shape=[
            jax.ShapeDtypeStruct((half * length * 4, LANES), F32),
            jax.ShapeDtypeStruct((2 * length, 4 * LANES), BF16),
            index,
            index,
        ],
        in_specs=[vmem, vmem, pl.BlockSpec(memory_space=pl.ANY)],
        out_specs=[vmem] * 4,
        scratch_shapes=[
            pltpu.VMEM(psi_v.shape, F32),
            pltpu.VMEM((pair_count, planes, plane_size), BF16),
            pltpu.VMEM(((half + half % 2) * 8, 6 * LANES), BF16),
            pltpu.VMEM((2 * length, 6 * length), BF16),
            pltpu.VMEM((2, pair_count * planes, LANES), F32),
            pltpu.VMEM((2, pair_count * planes, LANES), F32),
            pltpu.VMEM((half, 2 * length, 2 * LANES), F32),
            pltpu.SMEM((extra, 1, width), jnp.int32),
            pltpu.SemaphoreType.DMA((pair_count + 1,)),
        ],
        compiler_params=pltpu.CompilerParams(vmem_limit_bytes=40 * 2**20),
        name="transform",
    )(meta, psi_v, psi_c)


def landing(chip, chips):
    return chip * 2 % chips + chip // (chips // 2)


def points_kernel(length, pair_count, width, orders, spot, phase, plane, coef, pick, *refs):
    *refs, tiles_0, tiles_1, peak, local, sems = refs
    outs = refs[-max(len(orders), 1) :]
    me = lax.axis_index("fft")
    blocks, rows = outs[0].shape[0], outs[0].shape[1]
    last = blocks * len(outs) - 1
    chunked = len(orders) > 0
    which = lax.broadcasted_iota(jnp.int32, (2 * length, width), 0) % length

    def index_of(block):
        if not chunked:
            return block
        group, block = block // blocks, block % blocks
        far, across = (
            sum(jnp.where(group == k, order[axis], 0) for k, order in enumerate(orders)) for axis in range(2)
        )
        half = lax.rem(lax.rem(me, 2) + far, 2)
        chips = phase.shape[0] // 2
        return half * chips + landing(jnp.bitwise_xor(me // 2, 2 * block + across), chips)

    def fetch(block):
        return pltpu.make_async_copy(spot.at[index_of(block)], local.at[block], sems.at[block])

    def gather(block, tiles):
        for start in range(0, width, UNROLL):
            loaded = [plane[local[block, 0, start + u]] for u in range(UNROLL)]
            for u in range(UNROLL):
                tiles[(start + u) * 4 : (start + u + 1) * 4, :] = loaded[u]

    def combine(group, block, tiles):
        out = outs[group]
        turns = phase[index_of(group * blocks + block)]
        one_hot = jnp.where(which == turns % length, 1.0, 0.0).astype(BF16)
        factors = lax.dot_general(
            one_hot, coef[...], (((0,), (0,)), ((), ())), preferred_element_type=F32
        )
        cos = [factors[:, k * LANES : (k + 1) * LANES] for k in range(2)]
        sin = [factors[:, (k + 2) * LANES : (k + 3) * LANES] for k in range(2)]
        real = [tiles[pl.ds(k, width, stride=4), :] for k in range(2)]
        imag = [tiles[pl.ds(k + 2, width, stride=4), :] for k in range(2)]
        sums = (
            cos[0] * real[0] + sin[0] * imag[0] + (cos[1] * real[1] + sin[1] * imag[1]),
            cos[0] * imag[0] - sin[0] * real[0] + (cos[1] * imag[1] - sin[1] * real[1]),
        )
        sign = jnp.where(turns >= length, -1.0, 1.0)
        for to_imag in range(2):
            high, low = split(sums[to_imag])
            result = dot_nt(pick[...], jnp.concatenate([high, low], 1))
            if to_imag:
                result = result * sign
            if not chunked:
                out[block, to_imag * pair_count : (to_imag + 1) * pair_count, :] = result
                continue
            for k in range(width // LANES):
                start = (2 * k + to_imag) * pair_count
                tile = result[:, k * LANES : (k + 1) * LANES]
                out[block, start : start + pair_count, :] = tile
                peak[...] = jnp.maximum(peak[...], jnp.abs(tile))

    for block in range(last + 1):
        fetch(block).start()
    peak[...] = jnp.zeros_like(peak)
    tiles = (tiles_0, tiles_1)
    if chunked:
        for block in range(last + 2):
            if block <= last:
                fetch(block).wait()
                gather(block, tiles[block % 2])
            if block > 0:
                combine((block - 1) // blocks, (block - 1) % blocks, tiles[(block - 1) % 2])
    else:
        for block in range(last + 1):
            fetch(block).wait()
        gather(0, tiles_0)

        def two_blocks(step, _):
            gather(2 * step + 1, tiles_1)
            combine(0, 2 * step, tiles_0)
            gather(jnp.minimum(2 * step + 2, last), tiles_0)
            combine(0, 2 * step + 1, tiles_1)
            return 0

        lax.fori_loop(0, blocks // 2, two_blocks, 0)
    if chunked:
        used = width // LANES * 2 * pair_count
        top = jnp.broadcast_to(jnp.max(peak[...], axis=0, keepdims=True), (rows - used, LANES))
        for out in outs:
            for block in range(blocks):
                out[block, used:, :] = top


def points(spot, phase, plane, coef, pick, pair_count, out_shape, orders, after):
    after = () if after is None else (after,)
    count = max(len(orders), 1)
    length, width = coef.shape[0] // 2, phase.shape[2]
    vmem = pl.BlockSpec(memory_space=pltpu.VMEM)
    hbm = pl.BlockSpec(memory_space=pl.ANY)
    return pl.pallas_call(
        functools.partial(points_kernel, length, pair_count, width, orders),
        out_shape=[jax.ShapeDtypeStruct(out_shape, F32)] * count,
        in_specs=[hbm] + [vmem] * 4 + [hbm] * len(after),
        out_specs=[vmem] * count,
        scratch_shapes=[
            pltpu.VMEM((width * 4, LANES), F32),
            pltpu.VMEM((width * 4, LANES), F32),
            pltpu.VMEM((pair_count, LANES), F32),
            pltpu.SMEM((count * out_shape[0], 1, width), jnp.int32),
            pltpu.SemaphoreType.DMA((count * out_shape[0],)),
        ],
        compiler_params=pltpu.CompilerParams(vmem_limit_bytes=12 * 2**20),
        cost_estimate=pl.CostEstimate(flops=10**8 * out_shape[0], bytes_accessed=2**20, transcendentals=0),
        name="points",
    )(spot, phase, plane, coef, pick, *after)


def sphere_parts(psi_v, psi_c, pair_v, pair_c, g_index, devices, paired):
    pair_count = pair_v.shape[0]
    width = g_index.shape[0] // devices
    filling = jnp.zeros(-(g_index.shape[0] + 2 * pair_count) % math.lcm(width, 1024), jnp.int32)
    meta = jnp.concatenate([g_index, pair_v, pair_c, filling]).reshape(-1, 1, width)
    plane, coef, spot, phase = transform(psi_v, psi_c, meta, pair_count, devices)
    pick = (np.arange(2 * LANES)[None, :] % SLOT == np.arange(pair_count)[:, None]).astype(jnp.bfloat16)
    rest = (spot, phase, plane.reshape(-1, 4, LANES), coef, pick, pair_count)
    if not paired:
        return points(*rest, (devices, 2 * pair_count, width), (), None)[0]
    shape = (devices // 4, width // LANES * 2 * pair_count + 8, LANES)
    return [functools.partial(points, *rest, shape, orders) for orders in (((1, 1),), ((0, 1),), ((1, 0), (0, 0)))]


def chi_kernel(groups, pair_count, first, rows, cols, real, imag, left):
    width = rows.shape[1]

    @pl.when(pl.program_id(0) == 0)
    def _():
        own = rows[...].astype(F32)
        cross = []
        for group in range(groups):
            start = group * 2 * pair_count
            cross.append(-own[start + pair_count : start + 2 * pair_count])
            cross.append(own[start : start + pair_count])
        left[:width] = (-own).T.astype(BF16)
        left[width:] = jnp.concatenate(cross, 0).T.astype(BF16)

    for k in range(cols.shape[0]):
        both = jnp.dot(left[...], cols[k], preferred_element_type=F32)
        real[:, k * width : (k + 1) * width] = both[:width]
        imag[:, k * width : (k + 1) * width] = both[width:]


def chi_blocks(rows, cols, first, blocks, groups, pair_count):
    depth, width = rows.shape
    out = jax.ShapeDtypeStruct((width, blocks * width), F32)
    step = LANES // math.gcd(width, LANES)
    out_spec = pl.BlockSpec((width, step * width), lambda j, first: (0, j))
    return pl.pallas_call(
        functools.partial(chi_kernel, groups, pair_count),
        out_shape=(out, out),
        grid_spec=pltpu.PrefetchScalarGridSpec(
            num_scalar_prefetch=1,
            grid=(blocks // step,),
            in_specs=[
                pl.BlockSpec((depth, width), lambda j, first: (0, 0)),
                pl.BlockSpec((step, depth, width), lambda j, first: (first[0] // step + j, 0, 0)),
            ],
            out_specs=(out_spec, out_spec),
            scratch_shapes=[pltpu.VMEM((2 * width, depth), BF16)],
        ),
        compiler_params=pltpu.CompilerParams(vmem_limit_bytes=32 * 2**20),
        name="chi",
    )(first, rows, cols)


def chi_direct_kernel(pair_count, width, shifts, has_left, *refs):
    depth = 2 * pair_count
    chunks = width // LANES
    wide = lambda piece: jnp.concatenate([piece[k * depth : (k + 1) * depth] for k in range(chunks)], 1)
    chip, chips = lax.axis_index("fft") // 2, lax.axis_size("fft") // 2
    if has_left:
        left, refs = refs[0], refs[3:]
        *cols, real, imag, stage, sems = refs
    else:
        row_refs, refs = refs[:2], refs[2:]
        *cols, real, imag, left, stage, sems = refs
        own = [wide(piece[...].astype(F32)) for piece in row_refs]
        cross = [part for piece in own for part in (-piece[pair_count:], piece[:pair_count])]
        left[:width] = (-jnp.concatenate(own, 0)).T.astype(BF16)
        left[width:] = jnp.concatenate(cross, 0).T.astype(BF16)

    def copies(s):
        block = landing(jnp.bitwise_xor(chip, shifts[s]), chips)
        start = pl.multiple_of(block * width, LANES)
        return [
            pltpu.make_async_copy(
                stage.at[s, pl.ds(i * width, width)], out.at[:, pl.ds(start, width)], sems.at[s, i]
            )
            for i, out in enumerate((real, imag))
        ]

    s = 0
    for own_pairs, other_pairs in zip(cols[::2], cols[1::2]):
        for start in range(0, own_pairs.shape[0], 2):
            rights = [
                jnp.concatenate([wide(own_pairs[k]), wide(other_pairs[k])], 0) for k in (start, start + 1)
            ]
            both = jnp.dot(left[...], jnp.concatenate(rights, 1), preferred_element_type=F32)
            for k in range(2):
                stage[s + k] = both[:, k * width : (k + 1) * width]
                for copy in copies(s + k):
                    copy.start()
            s += 2
    for s in range(len(shifts)):
        for copy in copies(s):
            copy.wait()


def chi_direct(rows, cols, shifts, done, pair_count, width, blocks):
    out = jax.ShapeDtypeStruct((width, blocks * width), F32)
    left = jax.ShapeDtypeStruct((2 * width, 4 * pair_count), BF16)
    vmem = pl.BlockSpec(memory_space=pltpu.VMEM)
    hbm = pl.BlockSpec(memory_space=pl.ANY)
    if done is None:
        args, specs, aliases = rows, [vmem, vmem], {}
        out_shape, out_specs = (out, out, left), (hbm, hbm, vmem)
    else:
        real, imag, left = done
        args, specs, aliases = (left, real, imag), [vmem, hbm, hbm], {1: 0, 2: 1}
        out_shape, out_specs = (out, out), (hbm, hbm)
    cols = [array for pair in cols for array in pair]
    count = len(shifts)
    return pl.pallas_call(
        functools.partial(chi_direct_kernel, pair_count, width, shifts, done is not None),
        out_shape=out_shape,
        in_specs=specs + [vmem] * len(cols),
        out_specs=out_specs,
        scratch_shapes=[
            pltpu.VMEM((count, 2 * width, width), F32),
            pltpu.SemaphoreType.DMA((count, 2)),
        ],
        input_output_aliases=aliases,
        compiler_params=pltpu.CompilerParams(vmem_limit_bytes=32 * 2**20),
        cost_estimate=pl.CostEstimate(flops=1, bytes_accessed=1, transcendentals=0),
        name="chi",
    )(*args, *cols)


def pair_factor(energy_v, energy_c, pair_v, pair_c, length):
    chosen = lambda table, which: jnp.sum(
        jnp.where(which[:, None] == jnp.arange(table.shape[0])[None, :], table[None, :], 0.0), 1
    )
    weight = 2.0 / (chosen(energy_c, pair_c) - chosen(energy_v, pair_v))
    return jnp.sqrt(weight) * (pair_v.shape[0] * lax.axis_size("grp")) ** (-0.25) * length ** (-1.5)


def permute(values, moves):
    chips = lax.axis_size("fft") // 2
    perm = []
    for chip in range(chips):
        for core in range(2):
            for y in range(2):
                to_chip, to_core, to_y = moves(chip, core, y)
                perm.append((chip * 4 + core * 2 + y, to_chip * 4 + to_core * 2 + to_y))
    return lax.ppermute(values, ("fft", "grp"), perm)


def encode(values, used):
    top = values[..., used : used + 1, :]
    exponent = jnp.ceil(jnp.log2(jnp.maximum(top, 2.0**-100))) - 14.0
    row = lax.broadcasted_iota(jnp.int32, values.shape, values.ndim - 2)
    return jnp.where(row < used, values * jnp.exp2(-exponent), exponent).astype(jnp.float16)


def decode(coded, used):
    scale = jnp.exp2(coded[..., used : used + 1, :].astype(F32))
    row = lax.broadcasted_iota(jnp.int32, coded.shape, coded.ndim - 2)
    return jnp.where(row < used, coded.astype(F32), 2.0**14) * scale


def two_groups(psi_v, psi_c, energy_v, energy_c, pair_v, pair_c, g_index):
    devices = lax.axis_size("fft")
    chips = devices // 2
    quarter = chips // 2
    length = math.isqrt(psi_v.shape[2])
    pair_count = pair_v.shape[0]
    width = g_index.shape[0] // devices
    chunks = width // LANES
    used = chunks * 2 * pair_count
    fft, grp = lax.axis_index("fft"), lax.axis_index("grp")
    swap = lambda values: permute(values, lambda chip, core, y: (chip, 1 - core, y))
    swap_x = lambda values: permute(values, lambda chip, core, y: (chip ^ 1, core, y))

    calls = sphere_parts(psi_v, psi_c, pair_v, pair_c, g_index, devices, True)
    (far,) = calls[0](None)
    arrived = swap(far)
    (across,) = calls[1](far)
    across = across + arrived
    coded, across = lax.optimization_barrier((encode(across, used), across))
    arrived_x = swap_x(coded)
    far, kept = calls[2](across)
    arrived_x, far = lax.optimization_barrier((arrived_x, far))
    kept = kept + swap(far) + decode(arrived_x, used)
    (pair_v, pair_c), kept = lax.optimization_barrier(((pair_v, pair_c), kept))
    factor = pair_factor(energy_v, energy_c, pair_v, pair_c, length)
    factor = jnp.tile(factor, 2 * chunks)[:, None]
    total = kept[0]
    for s in reversed(range(1, quarter)):
        move = lambda chip, core, y, s=s: (chip ^ (2 * s), core, y)
        total = total + decode(permute(encode(kept[s], used), move), used)
    own = (total[:used] * factor).astype(BF16)

    first = jnp.stack(
        [permute(own, lambda chip, core, y, s=s: (chip ^ (2 * s), y, core)) for s in range(quarter)]
    )
    first = lax.optimization_barrier(first)
    first_x = swap_x(first)
    halves = [first[: quarter // 2], first[quarter // 2 :]]
    second = [swap(half) for half in halves]

    def row_home(chip, core):
        return chip % quarter + core * quarter, chip // quarter

    same = permute(own, lambda chip, core, y: (*row_home(chip, core), y))
    cross = permute(own, lambda chip, core, y: (*row_home(chip, core), 1 - y))
    agree = fft % 2 == grp
    rows = (jnp.where(agree, same, cross), jnp.where(agree, cross, same))
    shifts = [2 * s for s in range(quarter)]
    real, imag, left = chi_direct(rows, list(zip(halves, second)), shifts, None, pair_count, width, chips)
    first_x, left = lax.optimization_barrier((first_x, left))
    shifts = [2 * s + 1 for s in range(quarter)]
    return chi_direct(None, [(first_x, swap(first_x))], shifts, (real, imag, left), pair_count, width, chips)


def any_groups(psi_v, psi_c, energy_v, energy_c, pair_v, pair_c, g_index):
    devices, groups = lax.axis_size("fft"), lax.axis_size("grp")
    length = math.isqrt(psi_v.shape[2])
    pair_count = pair_v.shape[0]
    parts = sphere_parts(psi_v, psi_c, pair_v, pair_c, g_index, devices, False)
    factor = pair_factor(energy_v, energy_c, pair_v, pair_c, length)
    factor = jnp.concatenate([factor, factor])
    arrived = lax.all_to_all(parts, "fft", split_axis=0, concat_axis=0, tiled=True)
    own = (jnp.sum(arrived, 0) * factor[:, None]).astype(BF16)
    rows = lax.all_gather(own, "grp", axis=0, tiled=True)
    cols = lax.all_gather(rows, "fft", axis=0, tiled=False)
    blocks = devices // groups
    first = (lax.axis_index("grp") * blocks).astype(jnp.int32).reshape(1)
    return chi_blocks(rows, cols, first, blocks, groups, pair_count)


def per_device(
    psi_valence,
    psi_conduction,
    energy_valence,
    energy_conduction,
    pair_valence,
    pair_conduction,
    g_index,
):
    args = (
        psi_valence,
        psi_conduction,
        energy_valence,
        energy_conduction,
        pair_valence,
        pair_conduction,
        g_index,
    )
    devices = lax.axis_size("fft")
    chips = devices // 2
    power_of_two = devices % 2 == 0 and chips & (chips - 1) == 0
    if lax.axis_size("grp") == 2 and power_of_two and chips >= 4 and g_index.shape[0] % (devices * LANES) == 0:
        return two_groups(*args)
    return any_groups(*args)


def solution(mesh):
    placed = (P(None, "fft", None), P(None, "fft", None), P(), P(), P("grp"), P("grp"), P())
    return jax.shard_map(
        per_device,
        mesh=mesh,
        in_specs=placed,
        out_specs=(P("fft", "grp"), P("fft", "grp")),
        check_vma=False,
    )
```
